32 devices in a mesh: dp: 2 (over x), lat: 16 (over z, y, core).
Axes of the slice: x: 2, y: 2, z: 4, core: 2. Of those that a mesh axis runs over, the one named last changes fastest.
Arguments:
- states: bfloat16 [2, 64, 128, 128], P('dp', 'lat'), may hold values from -6 to 6
- basis_table: bfloat16 [64, 25, 9, 5], replicated, may hold values from -1.1953125 to 1.1953125
- offsets: int32 [64], replicated, may hold values from -12 to -8, as said below
- widths: int32 [64], replicated, may hold values from 21 to 25, as said below
- mixing: bfloat16 [9, 128, 128], replicated, may hold values from -0.1875 to 0.1875
- cotangent: bfloat16 [2, 64, 128, 128], P('dp', 'lat'), may hold values from -6 to 6
Outputs:
- output: bfloat16 [2, 64, 128, 128], P('dp', 'lat')
- grad_states: bfloat16 [2, 64, 128, 128], P('dp', 'lat')
- grad_mixing: float32 [9, 128, 128], replicated
The draws below stay inside these ranges and needn't reach their ends.
Inputs may be any that keep to these rules, and one draw needn't show every extreme that they name: The support of every output latitude o contains o itself and lies within latitudes o - 12 to o + 12, so offsets[o] is at most 13 - widths[o]. widths is 25 at the two pole latitudes 0 and 63.
All inputs are finite; a program needn't handle non-finite values.
Results may differ from the reference program's by a relative error of at most 0.0049.
Values may be sent and summed in bfloat16 or wider, within the bound.
A program may use at most 64 MiB of HBM per device.

```python
import math
import jax
import jax.numpy as jnp
from jax import lax

BAND_ROWS = 4
LONGITUDES = 128
CHANNELS = 128
BASIS = 9
TAPS = 5
HALO = 12
SUPPORT = 25
LATITUDES = 64
SAMPLES = 2
N_LAT = 16


def support_table(key):
    support = 2 * HALO + 1
    latitude_ids = jnp.arange(LATITUDES, dtype=jnp.int32)
    distance = jnp.minimum(latitude_ids, LATITUDES - 1 - latitude_ids)
    jitter = jax.random.randint(jax.random.fold_in(key, 11), (LATITUDES,), 0, 5, dtype=jnp.int32)
    widths = support - jitter
    widths = jnp.where(distance == 0, support, widths)
    widths = jnp.where(latitude_ids == LATITUDES // 2, support - 4, widths)
    nudge = jax.random.randint(jax.random.fold_in(key, 23), (LATITUDES,), -1, 2, dtype=jnp.int32)
    centred = -(widths // 2) + nudge
    offsets = jnp.clip(centred, -HALO, HALO - widths + 1)
    offsets = jnp.minimum(offsets, 0)
    highest = min(0, 4 - HALO)
    offsets = jnp.where(latitude_ids == LATITUDES // 2, highest, offsets)
    return (offsets.astype(jnp.int32), widths.astype(jnp.int32))


def draw_offsets(key, part):
    return support_table(key)[0]


def draw_widths(key, part):
    return support_table(key)[1]


def level_of(rng, shape, split, smallest, top_value):
    factor_of = 1.0
    for dim, parts in split:
        draws = jax.random.uniform(jax.random.fold_in(jax.random.fold_in(rng, 6), dim), (parts,), jnp.float32, smallest / len(split), top_value / len(split))
        factor_of = factor_of * jnp.repeat(jnp.exp(draws), shape[dim] // parts).reshape((-1,) + (1,) * (len(shape) - 1 - dim))
    return factor_of


def noise(stream_key, extent, width, limit, split=(), held_as=jnp.bfloat16):
    array = width * jax.random.normal(stream_key, extent, jnp.float32)
    if split:
        array = array * level_of(stream_key, extent, split, -0.22, 0.18)
    return jnp.clip(array, -limit, limit).astype(held_as)


def setup_inputs(seed: int = 0) -> dict:
    keys = jax.random.split(jax.random.key(seed), 7)
    states = noise(keys[0], (SAMPLES, LATITUDES, LONGITUDES, CHANNELS), 1.0, 6.0, ((0, 2), (1, 16)))
    basis_table = noise(keys[1], (LATITUDES, SUPPORT, BASIS, TAPS), 0.2, 1.1953125)
    offsets = draw_offsets(jax.random.fold_in(keys[6], 71), 0)
    widths = draw_widths(jax.random.fold_in(keys[6], 71), 0)
    mixing = noise(keys[4], (BASIS, CHANNELS, CHANNELS), (BASIS * CHANNELS) ** -0.5, 0.1875)
    cotangent = noise(keys[5], (SAMPLES, LATITUDES, LONGITUDES, CHANNELS), 1.0, 6.0, ((0, 2), (1, 16)))
    return dict(states=states, basis_table=basis_table, offsets=offsets, widths=widths, mixing=mixing, cotangent=cotangent)


def band_matrix(table_rows, offsets, widths, ext_rows, offset_base):
    out_rows = offsets.shape[0]
    support = table_rows.shape[1]
    slot_ids = jnp.arange(support, dtype=jnp.int32)
    target = jnp.arange(out_rows, dtype=jnp.int32)[:, None] + offset_base + offsets[:, None] + slot_ids[None, :]
    column = jnp.arange(ext_rows, dtype=jnp.int32)
    matches = (target[:, :, None] == column[None, None, :]) & (slot_ids[None, :, None] < widths[:, None, None])
    return jnp.einsum('qskt,qse->ktqe', table_rows.astype(jnp.float32), matches.astype(jnp.float32)).astype(jnp.bfloat16)

def reference(states, basis_table, offsets, widths, mixing, cotangent):
    half_taps = TAPS // 2
    ext_rows = BAND_ROWS + 2 * HALO
    weights = mixing.astype(jnp.float32)

    def one_sample(carry, pair):
        sample_state, sample_cot = pair
        padded = jnp.pad(sample_state, ((HALO, HALO), (0, 0), (0, 0)))

        def one_band(inner, band_index):
            grad_pad, grad_sum = inner
            first_row = (band_index * BAND_ROWS).astype(jnp.int32)
            window = lax.dynamic_slice_in_dim(padded, first_row, ext_rows, 0)
            matrix = band_matrix(lax.dynamic_slice_in_dim(basis_table, first_row, BAND_ROWS, 0), lax.dynamic_slice_in_dim(offsets, first_row, BAND_ROWS, 0), lax.dynamic_slice_in_dim(widths, first_row, BAND_ROWS, 0), ext_rows, HALO)
            rolled = jnp.stack([jnp.roll(window, half_taps - tap_index, axis=1) for tap_index in range(TAPS)])
            filtered = jnp.einsum('ktqe,telc->kqlc', matrix.astype(jnp.float32), rolled.astype(jnp.float32)).astype(jnp.bfloat16)
            band_out = jnp.einsum('kqlc,kcd->qld', filtered.astype(jnp.float32), weights).astype(jnp.bfloat16)
            band_cot = lax.dynamic_slice_in_dim(sample_cot, first_row, BAND_ROWS, 0).astype(jnp.float32)
            grad_filtered = jnp.einsum('qld,kcd->kqlc', band_cot, weights).astype(jnp.bfloat16)
            grad_sum = grad_sum + jnp.einsum('kqlc,qld->kcd', filtered.astype(jnp.float32), band_cot)
            partial_value = jnp.zeros((ext_rows, LONGITUDES, CHANNELS), jnp.float32)
            for tap_index in range(TAPS):
                term = jnp.einsum('kqe,kqlc->elc', matrix[:, tap_index].astype(jnp.float32), grad_filtered.astype(jnp.float32))
                partial_value = partial_value + jnp.roll(term, tap_index - half_taps, axis=1)
            current = lax.dynamic_slice_in_dim(grad_pad, first_row, ext_rows, 0)
            grad_pad = lax.dynamic_update_slice_in_dim(grad_pad, current + partial_value, first_row, 0)
            return ((grad_pad, grad_sum), band_out)
        grad_start = jnp.zeros((LATITUDES + 2 * HALO, LONGITUDES, CHANNELS), jnp.float32)
        (grad_pad, grad_sum), bands = lax.scan(one_band, (grad_start, carry), jnp.arange(N_LAT, dtype=jnp.int32))
        sample_out = bands.reshape(LATITUDES, LONGITUDES, CHANNELS)
        sample_grad = grad_pad[HALO:HALO + LATITUDES].astype(jnp.bfloat16)
        return (grad_sum, (sample_out, sample_grad))
    total_start = jnp.zeros((BASIS, CHANNELS, CHANNELS), jnp.float32)
    total, (output, grad_states) = lax.scan(one_sample, total_start, (states, cotangent))
    grad_mixing = total * (1.0 / math.sqrt(SAMPLES * LATITUDES * LONGITUDES))
    return (output, grad_states, grad_mixing)
```

```python
import functools
import math

import numpy as np
import jax
import jax.numpy as jnp
from jax import lax
from jax.experimental import pallas as pl
from jax.experimental.pallas import tpu as pltpu
from jax.sharding import PartitionSpec as P

HALO = 12
LB = 4
PLANE_DP = 2
PLANE_LAT = 4
MESH = pl.DeviceIdType.MESH
BF = jnp.bfloat16
F32 = jnp.float32


def dot(a, b):
    return jnp.dot(a, b, preferred_element_type=F32)


def structure(rows, basis, taps):
    ext = rows + 2 * HALO
    hops = ext // rows
    win = LB + taps - 1
    place = np.full((8, 256), -100000, np.int32)
    for r in range(rows):
        for e in range(ext):
            p = r * ext + e
            place[0, p] = r
            place[1, p] = e - r - HALO
            place[0, 128 + p] = e - HALO
            place[1, 128 + p] = r + HALO - e
    band = basis * LB * rows
    expand = np.zeros((taps, band, basis * taps), np.float32)
    own = np.zeros((band, 256), np.float32)
    spread = np.zeros((128, hops * win * rows), np.float32)
    tap = np.zeros((taps, band, hops * win * rows), np.float32)
    for k in range(basis):
        for lp in range(LB):
            for r in range(rows):
                row = (k * LB + lp) * rows + r
                for t in range(taps):
                    expand[t, row, k * taps + t] = 1
                    for j in range(hops):
                        base = (j * win + lp + t) * rows
                        tap[t, row, base : base + rows] = 1
                own[row, r * ext : (r + 1) * ext] = 1
                own[row, 128 + r * ext : 128 + (r + 1) * ext] = 1
    for r in range(rows):
        for e in range(ext):
            for w in range(win):
                spread[r * ext + e, ((e // rows) * win + w) * rows + e % rows] = 1
    as_bf = lambda x: np.asarray(x, dtype=jnp.bfloat16)
    return place, as_bf(expand), as_bf(own), as_bf(spread), as_bf(tap)


def kernel(
    n_dp, n_lat,
    states, cot, table, offs, wids, mixing, place, expand, own, spread, tap,
    out, grad_states, grad_mix,
    buf_s, buf_c, rt, band_f, band_a, mix_t, filt, send_a, recv_a, part_b, recv_b, chunk, full,
    halo_send, halo_recv, a_send, a_recv, b_send, b_recv, d_send, d_recv,
):
    rows, lons, chans = states.shape
    basis = mixing.shape[0]
    taps = table.shape[0] // basis
    hops = buf_s.shape[0]
    reach = hops // 2
    n_plane = PLANE_DP * PLANE_LAT
    n_rest = (n_dp // PLANE_DP) * (n_lat // PLANE_LAT)
    lat_rest = n_lat // PLANE_LAT
    dp = lax.axis_index("dp")
    lat = lax.axis_index("lat")
    g = (dp % PLANE_DP) * PLANE_LAT + lat % PLANE_LAT
    z = (dp // PLANE_DP) * lat_rest + lat // PLANE_LAT

    def plane_peer(m):
        h = (g + m) % n_plane
        return h, ((dp // PLANE_DP) * PLANE_DP + h // PLANE_LAT,
                   (lat // PLANE_LAT) * PLANE_LAT + h % PLANE_LAT)

    def rest_peer(m):
        h = (z + m) % n_rest
        return h, ((h // lat_rest) * PLANE_DP + dp % PLANE_DP,
                   (h % lat_rest) * PLANE_LAT + lat % PLANE_LAT)

    dists = [d for a in range(1, reach + 1) for d in (a, -a)]

    def there(d):
        return (lat + d >= 0) & (lat + d < n_lat)

    barrier = pltpu.get_barrier_semaphore()
    for d in dists:
        @pl.when(there(d))
        def _():
            pl.semaphore_signal(barrier, inc=1, device_id=(dp, lat + d), device_id_type=MESH)
    for m in range(1, n_plane):
        pl.semaphore_signal(barrier, inc=1, device_id=plane_peer(m)[1], device_id_type=MESH)
    for m in range(1, n_rest):
        pl.semaphore_signal(barrier, inc=1, device_id=rest_peer(m)[1], device_id_type=MESH)

    half = taps // 2
    wrapped = buf_s.shape[1]
    cells = rows * lons
    r_i = lax.broadcasted_iota(jnp.int32, (wrapped, cells), 0)
    c_i = lax.broadcasted_iota(jnp.int32, (wrapped, cells), 1)
    source = (r_i % rows) * lons + (r_i // rows - half + lons) % lons
    perm = (source == c_i).astype(F32).astype(BF)
    buf_s[reach] = dot(perm, states[...].reshape(cells, chans)).astype(BF)
    buf_c[reach] = dot(perm, cot[...].reshape(cells, chans)).astype(BF)

    near = sum(there(d).astype(jnp.int32) for d in dists)
    pl.semaphore_wait(barrier, near + (n_plane - 1 + n_rest - 1))

    def halo_copy(which, buf, d):
        return pltpu.make_async_remote_copy(
            src_ref=buf.at[reach], dst_ref=buf.at[reach - d],
            send_sem=halo_send.at[which, reach + d], recv_sem=halo_recv.at[which, reach - d],
            device_id=(dp, lat + d), device_id_type=MESH)

    def halo_arrival(which, buf, d):
        return pltpu.make_async_remote_copy(
            src_ref=buf.at[reach], dst_ref=buf.at[reach + d],
            send_sem=halo_send.at[which, reach + d], recv_sem=halo_recv.at[which, reach + d],
            device_id=(dp, lat + d), device_id_type=MESH)

    for which, buf in ((0, buf_s), (1, buf_c)):
        for d in dists:
            @pl.when(there(d))
            def _():
                halo_copy(which, buf, d).start()

            @pl.when(jnp.logical_not(there(d)))
            def _():
                buf[reach + d] = jnp.zeros(buf.shape[1:], BF)

    first = lat * rows
    n_o = table.shape[2]
    support = table.shape[1]
    o_i = lax.broadcasted_iota(jnp.int32, (n_o, 256), 0)
    pick = (o_i == place[0:1, :] + first).astype(F32).astype(BF)
    both = jnp.concatenate(
        [jnp.broadcast_to(offs[...].astype(F32), (8, n_o)),
         jnp.broadcast_to(wids[...].astype(F32), (8, n_o))], axis=0).astype(BF)
    picked = dot(both, pick)
    slot = place[1:2, :].astype(F32) - picked[0:1, :]
    s_i = lax.broadcasted_iota(jnp.int32, (support, 256), 0).astype(F32)
    live = jnp.where((s_i == slot) & (s_i < picked[8:9, :]), 1.0, 0.0)
    for kt in range(basis * taps):
        rt[kt : kt + 1, :] = jnp.sum(dot(table[kt], pick) * live, axis=0, keepdims=True)
    entries = rt[...].astype(BF)
    sum_f = jnp.zeros(band_f.shape, F32)
    sum_a = jnp.zeros(band_a.shape, F32)
    for t in range(taps):
        rows_t = (dot(expand[t], entries) * own[...].astype(F32)).astype(BF)
        sum_f = sum_f + dot(rows_t[:, :128], spread[...]) * tap[t].astype(F32)
        sum_a = sum_a + dot(rows_t[:, 128:], spread[...]) * tap[taps - 1 - t].astype(F32)
    band_f[...] = sum_f.astype(BF)
    band_a[...] = sum_a.astype(BF)
    for k in range(basis):
        mix_t[k * chans : (k + 1) * chans, :] = mixing[k].astype(F32).T.astype(BF)

    step = LB * rows
    span = (LB + taps - 1) * rows
    n_blocks = lons // LB

    def filter_all(band, buf):
        for b in range(0, n_blocks, 2):
            window = jnp.concatenate(
                [jnp.concatenate([buf[j, (b + i) * step : (b + i) * step + span, :]
                                  for j in range(hops)], axis=0) for i in range(2)], axis=1)
            res = dot(band[...], window).astype(BF)
            for i in range(2):
                for k in range(basis):
                    filt[(b + i) * step : (b + i + 1) * step, k * chans : (k + 1) * chans] = (
                        res[k * step : (k + 1) * step, i * chans : (i + 1) * chans])

    u_r = lax.broadcasted_iota(jnp.int32, (cells, cells), 0)
    u_c = lax.broadcasted_iota(jnp.int32, (cells, cells), 1)
    unperm = ((u_r % lons) * rows + u_r // lons == u_c).astype(F32).astype(BF)

    def wait_halo(which, buf):
        for d in dists:
            @pl.when(there(d))
            def _():
                halo_arrival(which, buf, d).wait_recv()

    wait_halo(0, buf_s)
    filter_all(band_f, buf_s)
    mid = half * rows
    cot_rows = buf_c[reach, mid : mid + cells, :]
    grad_t = dot(cot_rows.astype(F32).T.astype(BF), filt[...])
    for k in range(basis):
        send_a[k * chans : (k + 1) * chans, :] = grad_t[:, k * chans : (k + 1) * chans].T.astype(BF)
    piece = chunk.shape[0]

    def a_copy(m):
        h, peer = plane_peer(m)
        return pltpu.make_async_remote_copy(
            src_ref=send_a.at[pl.ds(pl.multiple_of(h * piece, 16), piece)], dst_ref=recv_a.at[m],
            send_sem=a_send.at[m], recv_sem=a_recv.at[m], device_id=peer, device_id_type=MESH)

    for m in range(1, n_plane):
        a_copy(m).start()

    mixed = dot(filt[...], mixing[...].reshape(basis * chans, chans)).astype(BF)
    out[...] = dot(unperm, mixed).astype(BF).reshape(out.shape)

    wait_halo(1, buf_c)
    filter_all(band_a, buf_c)

    for m in range(1, n_plane):
        a_copy(m).wait_recv()
    total = send_a[pl.ds(pl.multiple_of(g * piece, 16), piece), :].astype(F32)
    for m in range(1, n_plane):
        total = total + recv_a[m].astype(F32)
    part_b[...] = total.astype(BF)
    recv_b[z] = total.astype(BF)

    def b_copy(m):
        return pltpu.make_async_remote_copy(
            src_ref=part_b, dst_ref=recv_b.at[z],
            send_sem=b_send.at[m], recv_sem=b_recv.at[m], device_id=rest_peer(m)[1],
            device_id_type=MESH)

    for m in range(1, n_rest):
        b_copy(m).start()

    back = dot(filt[...], mix_t[...]).astype(BF)
    grad_states[...] = dot(unperm, back).astype(BF).reshape(grad_states.shape)

    for m in range(1, n_rest):
        src = (z - m + n_rest) % n_rest
        pltpu.make_async_remote_copy(
            src_ref=part_b, dst_ref=recv_b.at[src],
            send_sem=b_send.at[m], recv_sem=b_recv.at[m], device_id=rest_peer(m)[1],
            device_id_type=MESH).wait_recv()
    total = recv_b[0].astype(F32)
    for h in range(1, n_rest):
        total = total + recv_b[h].astype(F32)
    chunk[...] = total.astype(BF)
    full[pl.ds(pl.multiple_of(g * piece, 16), piece), :] = total.astype(BF)

    def d_copy(m, owner):
        return pltpu.make_async_remote_copy(
            src_ref=chunk, dst_ref=full.at[pl.ds(pl.multiple_of(owner * piece, 16), piece)],
            send_sem=d_send.at[m], recv_sem=d_recv.at[m], device_id=plane_peer(m)[1],
            device_id_type=MESH)

    for m in range(1, n_plane):
        d_copy(m, g).start()
    for m in range(1, n_plane):
        d_copy(m, (g - m + n_plane) % n_plane).wait_recv()
    grad_mix[...] = full[...]

    for which, buf in ((0, buf_s), (1, buf_c)):
        for d in dists:
            @pl.when(there(d))
            def _():
                halo_copy(which, buf, d).wait_send()
    for m in range(1, n_plane):
        a_copy(m).wait_send()
        d_copy(m, g).wait_send()
    for m in range(1, n_rest):
        b_copy(m).wait_send()


def shards(n_dp, n_lat, states, basis_table, offsets, widths, mixing, cotangent):
    samples, rows, lons, chans = states.shape
    n_o, support, basis, taps = basis_table.shape
    hops = 1 + 2 * (HALO // rows)
    n_plane = PLANE_DP * PLANE_LAT
    n_rest = n_dp * n_lat // n_plane
    wrapped = (lons + taps - 1) * rows
    cells = rows * lons
    deep = basis * chans
    piece = deep // n_plane
    place, expand, own, spread, tap = structure(rows, basis, taps)
    table = jnp.transpose(basis_table, (2, 3, 1, 0)).reshape(basis * taps, support, n_o)
    vmem = pl.BlockSpec(memory_space=pltpu.VMEM)
    dma = pltpu.SemaphoreType.DMA
    out, grad_states, grad_mix = pl.pallas_call(
        functools.partial(kernel, n_dp, n_lat),
        out_shape=(
            jax.ShapeDtypeStruct((rows, lons, chans), BF),
            jax.ShapeDtypeStruct((rows, lons, chans), BF),
            jax.ShapeDtypeStruct((deep, chans), BF),
        ),
        in_specs=[vmem] * 11,
        out_specs=(vmem, vmem, vmem),
        scratch_shapes=[
            pltpu.VMEM((hops, wrapped, chans), BF),
            pltpu.VMEM((hops, wrapped, chans), BF),
            pltpu.VMEM((basis * taps, 256), F32),
            pltpu.VMEM(tap.shape[1:], BF),
            pltpu.VMEM(tap.shape[1:], BF),
            pltpu.VMEM((deep, chans), BF),
            pltpu.VMEM((cells, deep), BF),
            pltpu.VMEM((deep, chans), BF),
            pltpu.VMEM((n_plane, piece, chans), BF),
            pltpu.VMEM((piece, chans), BF),
            pltpu.VMEM((n_rest, piece, chans), BF),
            pltpu.VMEM((piece, chans), BF),
            pltpu.VMEM((deep, chans), BF),
            dma((2, hops)), dma((2, hops)),
            dma((n_plane,)), dma((n_plane,)),
            dma((n_rest,)), dma((n_rest,)),
            dma((n_plane,)), dma((n_plane,)),
        ],
        compiler_params=pltpu.CompilerParams(
            collective_id=0, has_side_effects=True, vmem_limit_bytes=48 * 1024 * 1024),
        cost_estimate=pl.CostEstimate(
            flops=2 * cells * deep * (3 * chans + 2 * 28 * taps),
            bytes_accessed=8 * cells * chans, transcendentals=0),
    )(states.reshape(rows, lons, chans), cotangent.reshape(rows, lons, chans), table,
      offsets.reshape(1, n_o), widths.reshape(1, n_o), mixing,
      place, expand, own, spread, tap)
    cell_count = samples * n_dp * rows * n_lat * lons
    grad_mixing = grad_mix.astype(F32).reshape(basis, chans, chans) * (1.0 / math.sqrt(cell_count))
    shape = states.shape
    return (out.reshape(shape), grad_states.reshape(shape), grad_mixing)


def solution(mesh):
    n_dp, n_lat = mesh.shape["dp"], mesh.shape["lat"]
    in_specs = (P("dp", "lat", None, None), P(), P(), P(), P(), P("dp", "lat", None, None))
    out_specs = (P("dp", "lat", None, None), P("dp", "lat", None, None), P())
    return jax.shard_map(functools.partial(shards, n_dp, n_lat), mesh=mesh, in_specs=in_specs,
                         out_specs=out_specs, check_vma=False)
```

```python
import functools
import math

import numpy as np
import jax
import jax.numpy as jnp
from jax import lax
from jax.experimental import pallas as pl
from jax.experimental.pallas import tpu as pltpu
from jax.sharding import PartitionSpec as P

HALO = 12
LB = 4
PLANE_DP = 2
PLANE_LAT = 4
MESH = pl.DeviceIdType.MESH
BF = jnp.bfloat16
F32 = jnp.float32


def dot(a, b):
    return jnp.dot(a, b, preferred_element_type=F32)


def structure(rows, basis, taps):
    ext = rows + 2 * HALO
    hops = ext // rows
    win = LB + taps - 1
    place = np.full((8, 256), -100000, np.int32)
    for r in range(rows):
        for e in range(ext):
            p = r * ext + e
            place[0, p] = r
            place[1, p] = e - r - HALO
            place[0, 128 + p] = e - HALO
            place[1, 128 + p] = r + HALO - e
    band = basis * LB * rows
    expand = np.zeros((taps, band, basis * taps), np.float32)
    own = np.zeros((band, 256), np.float32)
    spread = np.zeros((128, hops * win * rows), np.float32)
    tap = np.zeros((taps, band, hops * win * rows), np.float32)
    for k in range(basis):
        for lp in range(LB):
            for r in range(rows):
                row = (k * LB + lp) * rows + r
                for t in range(taps):
                    expand[t, row, k * taps + t] = 1
                    for j in range(hops):
                        base = (j * win + lp + t) * rows
                        tap[t, row, base : base + rows] = 1
                own[row, r * ext : (r + 1) * ext] = 1
                own[row, 128 + r * ext : 128 + (r + 1) * ext] = 1
    for r in range(rows):
        for e in range(ext):
            for w in range(win):
                spread[r * ext + e, ((e // rows) * win + w) * rows + e % rows] = 1
    as_bf = lambda x: np.asarray(x, dtype=jnp.bfloat16)
    return place, as_bf(expand), as_bf(own), as_bf(spread), as_bf(tap)


def kernel(
    n_dp, n_lat,
    states_h, cot_h, table_h, offs_h, wids_h, mixing_h, place_h, expand_h, own_h, spread_h, tap_h,
    out, grad_states, grad_mix,
    states, cot, table, offs, wids, mixing, place, expand, own, spread, tap, load,
    buf_s, buf_c, rt, band_f, band_a, mix_t, filt, send_a, recv_a, part_b, recv_b, chunk, full,
    halo_send, halo_recv, a_send, a_recv, b_send, b_recv, d_send, d_recv,
):
    rows, lons, chans = states.shape
    basis = mixing.shape[0]
    taps = table.shape[0] // basis
    hops = buf_s.shape[0]
    reach = hops // 2
    n_plane = PLANE_DP * PLANE_LAT
    n_rest = (n_dp // PLANE_DP) * (n_lat // PLANE_LAT)
    lat_rest = n_lat // PLANE_LAT
    dp = lax.axis_index("dp")
    lat = lax.axis_index("lat")
    g = (dp % PLANE_DP) * PLANE_LAT + lat % PLANE_LAT
    z = (dp // PLANE_DP) * lat_rest + lat // PLANE_LAT

    def plane_peer(m):
        h = (g + m) % n_plane
        return h, ((dp // PLANE_DP) * PLANE_DP + h // PLANE_LAT,
                   (lat // PLANE_LAT) * PLANE_LAT + h % PLANE_LAT)

    def rest_peer(m):
        h = (z + m) % n_rest
        return h, ((h // lat_rest) * PLANE_DP + dp % PLANE_DP,
                   (h % lat_rest) * PLANE_LAT + lat % PLANE_LAT)

    loads = [
        pltpu.make_async_copy(src, dst, load.at[i])
        for i, (src, dst) in enumerate((
            (states_h, states), (cot_h, cot), (place_h, place), (offs_h, offs), (wids_h, wids),
            (table_h, table), (expand_h, expand), (own_h, own), (spread_h, spread),
            (tap_h, tap), (mixing_h, mixing)))
    ]
    for copy in loads:
        copy.start()

    core = lat % 2
    to_sib = 1 - 2 * core
    third = 6 * core - 3

    def there(d):
        return (lat + d >= 0) & (lat + d < n_lat)

    barrier = pltpu.get_barrier_semaphore()
    pl.semaphore_signal(barrier, inc=1, device_id=(dp, lat + to_sib), device_id_type=MESH)
    for d in (2, -2, third):
        @pl.when(there(d))
        def _():
            pl.semaphore_signal(barrier, inc=1, device_id=(dp, lat + d), device_id_type=MESH)
    for m in range(1, n_plane):
        pl.semaphore_signal(barrier, inc=1, device_id=plane_peer(m)[1], device_id_type=MESH)
    for m in range(1, n_rest):
        pl.semaphore_signal(barrier, inc=1, device_id=rest_peer(m)[1], device_id_type=MESH)

    half = taps // 2
    wrapped = buf_s.shape[1]
    cells = rows * lons
    r_i = lax.broadcasted_iota(jnp.int32, (wrapped, cells), 0)
    c_i = lax.broadcasted_iota(jnp.int32, (wrapped, cells), 1)
    source = (r_i % rows) * lons + (r_i // rows - half + lons) % lons
    perm = (source == c_i).astype(F32).astype(BF)

    def hop(which, buf, kind):
        src, slot, d, got, sent_if, got_if = {
            0: (reach, reach - to_sib, to_sib, reach + to_sib, None, None),
            1: (reach, reach - 2, 2, reach - 2, there(2), there(-2)),
            2: (reach, reach + 2, -2, reach + 2, there(-2), there(2)),
            3: (reach, reach - third, third, reach + third, there(third), there(third)),
            4: (reach - 2, reach - 2 - to_sib, to_sib, reach - 2 + to_sib, there(-2),
                there(to_sib - 2)),
            5: (reach + 2, reach + 2 - to_sib, to_sib, reach + 2 + to_sib, there(2),
                there(to_sib + 2)),
        }[kind]

        def copy(at):
            return pltpu.make_async_remote_copy(
                src_ref=buf.at[src], dst_ref=buf.at[at], send_sem=halo_send.at[which, kind],
                recv_sem=halo_recv.at[which, kind], device_id=(dp, lat + d), device_id_type=MESH)

        def run(cond, f):
            if cond is None:
                f()
            else:
                pl.when(cond)(f)

        return (lambda: run(sent_if, lambda: copy(slot).start()),
                lambda: run(got_if, lambda: copy(got).wait_recv()),
                lambda: run(sent_if, lambda: copy(slot).wait_send()))

    loads[0].wait()
    buf_s[reach] = dot(perm, states[...].reshape(cells, chans)).astype(BF)
    near = 1 + sum(there(d).astype(jnp.int32) for d in (2, -2, third))
    pl.semaphore_wait(barrier, near + (n_plane - 1 + n_rest - 1))
    for kind in (1, 2, 3, 0):
        hop(0, buf_s, kind)[0]()
    loads[1].wait()
    buf_c[reach] = dot(perm, cot[...].reshape(cells, chans)).astype(BF)
    for kind in (1, 2, 3, 0):
        hop(1, buf_c, kind)[0]()
    for buf in (buf_s, buf_c):
        for d in range(-reach, reach + 1):
            if d:
                @pl.when(jnp.logical_not(there(d)))
                def _():
                    buf[reach + d] = jnp.zeros(buf.shape[1:], BF)
    for copy in loads[2:]:
        copy.wait()

    first = lat * rows
    n_o = table.shape[2]
    support = table.shape[1]
    o_i = lax.broadcasted_iota(jnp.int32, (n_o, 256), 0)
    pick = (o_i == place[0:1, :] + first).astype(F32).astype(BF)
    both = jnp.concatenate(
        [jnp.broadcast_to(offs[...].astype(F32), (8, n_o)),
         jnp.broadcast_to(wids[...].astype(F32), (8, n_o))], axis=0).astype(BF)
    picked = dot(both, pick)
    slot = place[1:2, :].astype(F32) - picked[0:1, :]
    s_i = lax.broadcasted_iota(jnp.int32, (support, 256), 0).astype(F32)
    live = jnp.where((s_i == slot) & (s_i < picked[8:9, :]), 1.0, 0.0)
    for kt in range(basis * taps):
        rt[kt : kt + 1, :] = jnp.sum(dot(table[kt], pick) * live, axis=0, keepdims=True)
    entries = rt[...].astype(BF)
    sum_f = jnp.zeros(band_f.shape, F32)
    sum_a = jnp.zeros(band_a.shape, F32)
    for t in range(taps):
        rows_t = (dot(expand[t], entries) * own[...].astype(F32)).astype(BF)
        sum_f = sum_f + dot(rows_t[:, :128], spread[...]) * tap[t].astype(F32)
        sum_a = sum_a + dot(rows_t[:, 128:], spread[...]) * tap[taps - 1 - t].astype(F32)
    band_f[...] = sum_f.astype(BF)
    band_a[...] = sum_a.astype(BF)
    for k in range(basis):
        mix_t[k * chans : (k + 1) * chans, :] = mixing[k].astype(F32).T.astype(BF)

    step = LB * rows
    span = (LB + taps - 1) * rows
    n_blocks = lons // LB

    def filter_all(band, buf):
        for b in range(0, n_blocks, 2):
            window = jnp.concatenate(
                [jnp.concatenate([buf[j, (b + i) * step : (b + i) * step + span, :]
                                  for j in range(hops)], axis=0) for i in range(2)], axis=1)
            res = dot(band[...], window).astype(BF)
            for i in range(2):
                for k in range(basis):
                    filt[(b + i) * step : (b + i + 1) * step, k * chans : (k + 1) * chans] = (
                        res[k * step : (k + 1) * step, i * chans : (i + 1) * chans])

    u_r = lax.broadcasted_iota(jnp.int32, (cells, cells), 0)
    u_c = lax.broadcasted_iota(jnp.int32, (cells, cells), 1)
    unperm = ((u_r % lons) * rows + u_r // lons == u_c).astype(F32).astype(BF)

    def pass_on(which, buf):
        for kind in (1, 2):
            hop(which, buf, kind)[1]()
        for kind in (4, 5):
            hop(which, buf, kind)[0]()

    def wait_rest(which, buf):
        for kind in (0, 3, 4, 5):
            hop(which, buf, kind)[1]()

    pass_on(0, buf_s)
    wait_rest(0, buf_s)
    filter_all(band_f, buf_s)
    pass_on(1, buf_c)
    mid = half * rows
    cot_rows = buf_c[reach, mid : mid + cells, :]
    grad_t = dot(cot_rows.astype(F32).T.astype(BF), filt[...])
    for k in range(basis):
        send_a[k * chans : (k + 1) * chans, :] = grad_t[:, k * chans : (k + 1) * chans].T.astype(BF)
    piece = chunk.shape[0]

    def a_copy(m):
        h, peer = plane_peer(m)
        return pltpu.make_async_remote_copy(
            src_ref=send_a.at[pl.ds(pl.multiple_of(h * piece, 16), piece)], dst_ref=recv_a.at[m],
            send_sem=a_send.at[m], recv_sem=a_recv.at[m], device_id=peer, device_id_type=MESH)

    for m in range(1, n_plane):
        a_copy(m).start()

    mixed = dot(filt[...], mixing[...].reshape(basis * chans, chans)).astype(BF)
    out[...] = dot(unperm, mixed).astype(BF).reshape(out.shape)

    wait_rest(1, buf_c)
    filter_all(band_a, buf_c)

    for m in range(1, n_plane):
        a_copy(m).wait_recv()
    total = send_a[pl.ds(pl.multiple_of(g * piece, 16), piece), :].astype(F32)
    for m in range(1, n_plane):
        total = total + recv_a[m].astype(F32)
    part_b[...] = total.astype(BF)
    recv_b[z] = total.astype(BF)

    def b_copy(m):
        return pltpu.make_async_remote_copy(
            src_ref=part_b, dst_ref=recv_b.at[z],
            send_sem=b_send.at[m], recv_sem=b_recv.at[m], device_id=rest_peer(m)[1],
            device_id_type=MESH)

    for m in range(1, n_rest):
        b_copy(m).start()

    back = dot(filt[...], mix_t[...]).astype(BF)
    grad_states[...] = dot(unperm, back).astype(BF).reshape(grad_states.shape)

    for m in range(1, n_rest):
        src = (z - m + n_rest) % n_rest
        pltpu.make_async_remote_copy(
            src_ref=part_b, dst_ref=recv_b.at[src],
            send_sem=b_send.at[m], recv_sem=b_recv.at[m], device_id=rest_peer(m)[1],
            device_id_type=MESH).wait_recv()
    total = recv_b[0].astype(F32)
    for h in range(1, n_rest):
        total = total + recv_b[h].astype(F32)
    chunk[...] = total.astype(BF)
    full[pl.ds(pl.multiple_of(g * piece, 16), piece), :] = total.astype(BF)

    def d_copy(m, owner):
        return pltpu.make_async_remote_copy(
            src_ref=chunk, dst_ref=full.at[pl.ds(pl.multiple_of(owner * piece, 16), piece)],
            send_sem=d_send.at[m], recv_sem=d_recv.at[m], device_id=plane_peer(m)[1],
            device_id_type=MESH)

    for m in range(1, n_plane):
        d_copy(m, g).start()
    for m in range(1, n_plane):
        d_copy(m, (g - m + n_plane) % n_plane).wait_recv()
    grad_mix[...] = full[...]

    for which, buf in ((0, buf_s), (1, buf_c)):
        for kind in range(6):
            hop(which, buf, kind)[2]()
    for m in range(1, n_plane):
        a_copy(m).wait_send()
        d_copy(m, g).wait_send()
    for m in range(1, n_rest):
        b_copy(m).wait_send()


def shards(n_dp, n_lat, states, basis_table, offsets, widths, mixing, cotangent):
    samples, rows, lons, chans = states.shape
    n_o, support, basis, taps = basis_table.shape
    hops = 1 + 2 * (HALO // rows)
    n_plane = PLANE_DP * PLANE_LAT
    n_rest = n_dp * n_lat // n_plane
    wrapped = (lons + taps - 1) * rows
    cells = rows * lons
    deep = basis * chans
    piece = deep // n_plane
    place, expand, own, spread, tap = structure(rows, basis, taps)
    table = jnp.transpose(basis_table, (2, 3, 1, 0)).reshape(basis * taps, support, n_o)
    operands = [states.reshape(rows, lons, chans), cotangent.reshape(rows, lons, chans), table,
                offsets.reshape(1, n_o), widths.reshape(1, n_o), mixing,
                place, expand, own, spread, tap]
    vmem = pl.BlockSpec(memory_space=pltpu.VMEM)
    dma = pltpu.SemaphoreType.DMA
    out, grad_states, grad_mix = pl.pallas_call(
        functools.partial(kernel, n_dp, n_lat),
        out_shape=(
            jax.ShapeDtypeStruct((rows, lons, chans), BF),
            jax.ShapeDtypeStruct((rows, lons, chans), BF),
            jax.ShapeDtypeStruct((deep, chans), BF),
        ),
        in_specs=[pl.BlockSpec(memory_space=pltpu.HBM)] * 11,
        out_specs=(vmem, vmem, vmem),
        scratch_shapes=[pltpu.VMEM(x.shape, x.dtype) for x in operands] + [
            dma((len(operands),)),
            pltpu.VMEM((hops, wrapped, chans), BF),
            pltpu.VMEM((hops, wrapped, chans), BF),
            pltpu.VMEM((basis * taps, 256), F32),
            pltpu.VMEM(tap.shape[1:], BF),
            pltpu.VMEM(tap.shape[1:], BF),
            pltpu.VMEM((deep, chans), BF),
            pltpu.VMEM((cells, deep), BF),
            pltpu.VMEM((deep, chans), BF),
            pltpu.VMEM((n_plane, piece, chans), BF),
            pltpu.VMEM((piece, chans), BF),
            pltpu.VMEM((n_rest, piece, chans), BF),
            pltpu.VMEM((piece, chans), BF),
            pltpu.VMEM((deep, chans), BF),
            dma((2, 6)), dma((2, 6)),
            dma((n_plane,)), dma((n_plane,)),
            dma((n_rest,)), dma((n_rest,)),
            dma((n_plane,)), dma((n_plane,)),
        ],
        compiler_params=pltpu.CompilerParams(
            collective_id=0, has_side_effects=True, vmem_limit_bytes=63 * 1024 * 1024),
        cost_estimate=pl.CostEstimate(
            flops=2 * cells * deep * (3 * chans + 2 * 28 * taps),
            bytes_accessed=8 * cells * chans, transcendentals=0),
    )(*operands)
    cell_count = samples * n_dp * rows * n_lat * lons
    grad_mixing = grad_mix.astype(F32).reshape(basis, chans, chans) * (1.0 / math.sqrt(cell_count))
    shape = states.shape
    return (out.reshape(shape), grad_states.reshape(shape), grad_mixing)


def solution(mesh):
    n_dp, n_lat = mesh.shape["dp"], mesh.shape["lat"]
    in_specs = (P("dp", "lat", None, None), P(), P(), P(), P(), P("dp", "lat", None, None))
    out_specs = (P("dp", "lat", None, None), P("dp", "lat", None, None), P())
    return jax.shard_map(functools.partial(shards, n_dp, n_lat), mesh=mesh, in_specs=in_specs,
                         out_specs=out_specs, check_vma=False)
```

```python
import functools
import math

import numpy as np
import jax
import jax.numpy as jnp
from jax import lax
from jax.experimental import pallas as pl
from jax.experimental.pallas import tpu as pltpu
from jax.sharding import PartitionSpec as P

HALO = 12
LB = 4
PLANE_DP = 2
PLANE_LAT = 4
MESH = pl.DeviceIdType.MESH
BF = jnp.bfloat16
F32 = jnp.float32


def dot(a, b):
    return jnp.dot(a, b, preferred_element_type=F32)


def structure(rows, basis, taps):
    ext = rows + 2 * HALO
    hops = ext // rows
    win = LB + taps - 1
    place = np.full((8, 256), -100000, np.int32)
    for r in range(rows):
        for e in range(ext):
            p = r * ext + e
            place[0, p] = r
            place[1, p] = e - r - HALO
            place[0, 128 + p] = e - HALO
            place[1, 128 + p] = r + HALO - e
    band = basis * LB * rows
    expand = np.zeros((taps, band, basis * taps), np.float32)
    own = np.zeros((band, 256), np.float32)
    spread = np.zeros((128, hops * win * rows), np.float32)
    tap = np.zeros((taps, band, hops * win * rows), np.float32)
    for k in range(basis):
        for lp in range(LB):
            for r in range(rows):
                row = (k * LB + lp) * rows + r
                for t in range(taps):
                    expand[t, row, k * taps + t] = 1
                    for j in range(hops):
                        base = (j * win + lp + t) * rows
                        tap[t, row, base : base + rows] = 1
                own[row, r * ext : (r + 1) * ext] = 1
                own[row, 128 + r * ext : 128 + (r + 1) * ext] = 1
    for r in range(rows):
        for e in range(ext):
            for w in range(win):
                spread[r * ext + e, ((e // rows) * win + w) * rows + e % rows] = 1
    as_bf = lambda x: np.asarray(x, dtype=jnp.bfloat16)
    return place, as_bf(expand), as_bf(own), as_bf(spread), as_bf(tap)


def kernel(
    n_dp, n_lat,
    states_h, cot_h, table_h, offs_h, wids_h, mixing_h, place_h, expand_h, own_h, spread_h, tap_h,
    out_h, grad_states_h, grad_mix_h,
    out, grad_states, store,
    states, cot, table, offs, wids, mixing, place, expand, own, spread, tap, load,
    buf_s, buf_c, rt, band_f, band_a, mix_t, filt, send_a, recv_a, part_b, recv_b, chunk, full,
    halo_send, halo_recv, a_send, a_recv, b_send, b_recv, d_send, d_recv,
):
    rows, lons, chans = states.shape
    basis = mixing.shape[0]
    taps = table.shape[0] // basis
    hops = buf_s.shape[0]
    reach = hops // 2
    n_plane = PLANE_DP * PLANE_LAT
    n_rest = (n_dp // PLANE_DP) * (n_lat // PLANE_LAT)
    lat_rest = n_lat // PLANE_LAT
    dp = lax.axis_index("dp")
    lat = lax.axis_index("lat")
    g = (dp % PLANE_DP) * PLANE_LAT + lat % PLANE_LAT
    z = (dp // PLANE_DP) * lat_rest + lat // PLANE_LAT

    def plane_peer(m):
        h = (g + m) % n_plane
        return h, ((dp // PLANE_DP) * PLANE_DP + h // PLANE_LAT,
                   (lat // PLANE_LAT) * PLANE_LAT + h % PLANE_LAT)

    def rest_peer(m):
        h = (z + m) % n_rest
        return h, ((h // lat_rest) * PLANE_DP + dp % PLANE_DP,
                   (h % lat_rest) * PLANE_LAT + lat % PLANE_LAT)

    loads = [
        pltpu.make_async_copy(src, dst, load.at[i])
        for i, (src, dst) in enumerate((
            (states_h, states), (cot_h, cot), (place_h, place), (offs_h, offs), (wids_h, wids),
            (table_h, table), (expand_h, expand), (own_h, own), (spread_h, spread),
            (tap_h, tap), (mixing_h, mixing)))
    ]
    for copy in loads:
        copy.start()

    core = lat % 2
    to_sib = 1 - 2 * core
    third = 6 * core - 3

    def there(d):
        return (lat + d >= 0) & (lat + d < n_lat)

    barrier = pltpu.get_barrier_semaphore()
    pl.semaphore_signal(barrier, inc=1, device_id=(dp, lat + to_sib), device_id_type=MESH)
    for d in (2, -2, third):
        @pl.when(there(d))
        def _():
            pl.semaphore_signal(barrier, inc=1, device_id=(dp, lat + d), device_id_type=MESH)
    for m in range(1, n_plane):
        pl.semaphore_signal(barrier, inc=1, device_id=plane_peer(m)[1], device_id_type=MESH)
    for m in range(1, n_rest):
        pl.semaphore_signal(barrier, inc=1, device_id=rest_peer(m)[1], device_id_type=MESH)

    half = taps // 2
    wrapped = buf_s.shape[1]
    cells = rows * lons
    rows_log, lons_log = rows.bit_length() - 1, lons.bit_length() - 1
    r_i = lax.broadcasted_iota(jnp.int32, (wrapped, cells), 0)
    c_i = lax.broadcasted_iota(jnp.int32, (wrapped, cells), 1)
    turned = jnp.where(r_i >= half * rows, r_i - half * rows, r_i + cells - half * rows)
    turned = jnp.where(turned >= cells, turned - cells, turned)
    source = (turned & (rows - 1)) * lons + (turned >> rows_log)
    perm = (source == c_i).astype(F32).astype(BF)

    def hop(which, buf, kind):
        src, slot, d, got, sent_if, got_if = {
            0: (reach, reach - to_sib, to_sib, reach + to_sib, None, None),
            1: (reach, reach - 2, 2, reach - 2, there(2), there(-2)),
            2: (reach, reach + 2, -2, reach + 2, there(-2), there(2)),
            3: (reach, reach - third, third, reach + third, there(third), there(third)),
            4: (reach - 2, reach - 2 - to_sib, to_sib, reach - 2 + to_sib, there(-2),
                there(to_sib - 2)),
            5: (reach + 2, reach + 2 - to_sib, to_sib, reach + 2 + to_sib, there(2),
                there(to_sib + 2)),
        }[kind]

        def copy(at):
            return pltpu.make_async_remote_copy(
                src_ref=buf.at[src], dst_ref=buf.at[at], send_sem=halo_send.at[which, kind],
                recv_sem=halo_recv.at[which, kind], device_id=(dp, lat + d), device_id_type=MESH)

        def run(cond, f):
            if cond is None:
                f()
            else:
                pl.when(cond)(f)

        return (lambda: run(sent_if, lambda: copy(slot).start()),
                lambda: run(got_if, lambda: copy(got).wait_recv()),
                lambda: run(sent_if, lambda: copy(slot).wait_send()))

    loads[0].wait()
    buf_s[reach] = dot(perm, states[...].reshape(cells, chans)).astype(BF)
    near = 1 + sum(there(d).astype(jnp.int32) for d in (2, -2, third))
    pl.semaphore_wait(barrier, near + (n_plane - 1 + n_rest - 1))
    for kind in (1, 2, 3, 0):
        hop(0, buf_s, kind)[0]()
    loads[1].wait()
    buf_c[reach] = dot(perm, cot[...].reshape(cells, chans)).astype(BF)
    for buf in (buf_s, buf_c):
        for d in range(-reach, reach + 1):
            if d:
                @pl.when(jnp.logical_not(there(d)))
                def _():
                    buf[reach + d] = jnp.zeros(buf.shape[1:], BF)
    for copy in loads[2:]:
        copy.wait()

    first = lat * rows
    n_o = table.shape[2]
    support = table.shape[1]
    o_i = lax.broadcasted_iota(jnp.int32, (n_o, 256), 0)
    pick = (o_i == place[0:1, :] + first).astype(F32).astype(BF)
    both = jnp.concatenate(
        [jnp.broadcast_to(offs[...].astype(F32), (8, n_o)),
         jnp.broadcast_to(wids[...].astype(F32), (8, n_o))], axis=0).astype(BF)
    picked = dot(both, pick)
    slot = place[1:2, :].astype(F32) - picked[0:1, :]
    s_i = lax.broadcasted_iota(jnp.int32, (support, 256), 0).astype(F32)
    live = jnp.where((s_i == slot) & (s_i < picked[8:9, :]), 1.0, 0.0)
    for kt in range(basis * taps):
        rt[kt : kt + 1, :] = jnp.sum(dot(table[kt], pick) * live, axis=0, keepdims=True)
    entries = rt[...].astype(BF)

    def build(band, lanes, tap_of):
        acc = jnp.zeros(band.shape, F32)
        for t in range(taps):
            rows_t = (dot(expand[t], entries[:, lanes]) * own[:, lanes].astype(F32)).astype(BF)
            acc = acc + dot(rows_t, spread[...]) * tap[tap_of(t)].astype(F32)
        band[...] = acc.astype(BF)

    build(band_f, slice(0, 128), lambda t: t)

    step = LB * rows
    span = (LB + taps - 1) * rows
    n_blocks = lons // LB

    def filter_all(band, buf):
        for b in range(0, n_blocks, 2):
            window = jnp.concatenate(
                [jnp.concatenate([buf[j, (b + i) * step : (b + i) * step + span, :]
                                  for j in range(hops)], axis=0) for i in range(2)], axis=1)
            res = dot(band[...], window).astype(BF)
            for i in range(2):
                for k in range(basis):
                    filt[(b + i) * step : (b + i + 1) * step, k * chans : (k + 1) * chans] = (
                        res[k * step : (k + 1) * step, i * chans : (i + 1) * chans])

    u_r = lax.broadcasted_iota(jnp.int32, (cells, cells), 0)
    u_c = lax.broadcasted_iota(jnp.int32, (cells, cells), 1)
    unperm = ((u_r & (lons - 1)) * rows + (u_r >> lons_log) == u_c).astype(F32).astype(BF)

    def pass_on(which, buf):
        for kind in (1, 2):
            hop(which, buf, kind)[1]()
        for kind in (4, 5):
            hop(which, buf, kind)[0]()

    def wait_rest(which, buf):
        for kind in (0, 3, 4, 5):
            hop(which, buf, kind)[1]()

    def unpermuted(x, ref):
        ref[...] = dot(unperm, x.astype(BF)).astype(BF).reshape(ref.shape)

    stores = [pltpu.make_async_copy(src, dst, store.at[i]) for i, (src, dst) in enumerate(
        ((out, out_h), (grad_states, grad_states_h), (full, grad_mix_h)))]

    pass_on(0, buf_s)
    for kind in (1, 2, 3, 0):
        hop(1, buf_c, kind)[0]()
    wait_rest(0, buf_s)
    filter_all(band_f, buf_s)
    mid = half * rows
    cot_rows = buf_c[reach, mid : mid + cells, :]
    grad_t = dot(cot_rows.astype(F32).T.astype(BF), filt[...])
    for k in range(basis):
        send_a[k * chans : (k + 1) * chans, :] = grad_t[:, k * chans : (k + 1) * chans].T.astype(BF)
    piece = chunk.shape[0]

    def a_copy(m):
        h, peer = plane_peer(m)
        return pltpu.make_async_remote_copy(
            src_ref=send_a.at[pl.ds(pl.multiple_of(h * piece, 16), piece)], dst_ref=recv_a.at[m],
            send_sem=a_send.at[m], recv_sem=a_recv.at[m], device_id=peer, device_id_type=MESH)

    for m in range(1, n_plane):
        a_copy(m).start()

    pass_on(1, buf_c)
    unpermuted(dot(filt[...], mixing[...].reshape(basis * chans, chans)), out)
    stores[0].start()
    build(band_a, slice(128, 256), lambda t: taps - 1 - t)
    for k in range(basis):
        mix_t[k * chans : (k + 1) * chans, :] = mixing[k].astype(F32).T.astype(BF)

    for m in range(1, n_plane):
        a_copy(m).wait_recv()
    total = send_a[pl.ds(pl.multiple_of(g * piece, 16), piece), :].astype(F32)
    for m in range(1, n_plane):
        total = total + recv_a[m].astype(F32)
    part_b[...] = total.astype(BF)
    recv_b[z] = total.astype(BF)

    def b_copy(m, owner):
        return pltpu.make_async_remote_copy(
            src_ref=part_b, dst_ref=recv_b.at[owner],
            send_sem=b_send.at[m], recv_sem=b_recv.at[m], device_id=rest_peer(m)[1],
            device_id_type=MESH)

    for m in range(1, n_rest):
        b_copy(m, z).start()

    wait_rest(1, buf_c)
    filter_all(band_a, buf_c)

    for m in range(1, n_rest):
        b_copy(m, (z - m + n_rest) % n_rest).wait_recv()
    total = recv_b[0].astype(F32)
    for h in range(1, n_rest):
        total = total + recv_b[h].astype(F32)
    chunk[...] = total.astype(BF)
    full[pl.ds(pl.multiple_of(g * piece, 16), piece), :] = total.astype(BF)

    def d_copy(m, owner):
        return pltpu.make_async_remote_copy(
            src_ref=chunk, dst_ref=full.at[pl.ds(pl.multiple_of(owner * piece, 16), piece)],
            send_sem=d_send.at[m], recv_sem=d_recv.at[m], device_id=plane_peer(m)[1],
            device_id_type=MESH)

    for m in range(1, n_plane):
        d_copy(m, g).start()

    unpermuted(dot(filt[...], mix_t[...]), grad_states)
    stores[1].start()

    for m in range(1, n_plane):
        d_copy(m, (g - m + n_plane) % n_plane).wait_recv()
    stores[2].start()

    for which, buf in ((0, buf_s), (1, buf_c)):
        for kind in range(6):
            hop(which, buf, kind)[2]()
    for m in range(1, n_plane):
        a_copy(m).wait_send()
        d_copy(m, g).wait_send()
    for m in range(1, n_rest):
        b_copy(m, z).wait_send()
    for copy in stores:
        copy.wait()


def finish(scale, out_in, grad_in, mix_in, out, grad_states, grad_mix, held, wide, sems):
    read = pltpu.make_async_copy(mix_in, held, sems.at[0])
    read.start()
    first = pltpu.make_async_copy(out_in, out, sems.at[1])
    second = pltpu.make_async_copy(grad_in, grad_states, sems.at[2])
    first.start()
    second.start()
    read.wait()
    wide[...] = held[...].astype(F32) * scale
    write = pltpu.make_async_copy(wide, grad_mix, sems.at[3])
    write.start()
    first.wait()
    second.wait()
    write.wait()


def shards(n_dp, n_lat, states, basis_table, offsets, widths, mixing, cotangent):
    samples, rows, lons, chans = states.shape
    n_o, support, basis, taps = basis_table.shape
    hops = 1 + 2 * (HALO // rows)
    n_plane = PLANE_DP * PLANE_LAT
    n_rest = n_dp * n_lat // n_plane
    wrapped = (lons + taps - 1) * rows
    cells = rows * lons
    deep = basis * chans
    piece = deep // n_plane
    place, expand, own, spread, tap = structure(rows, basis, taps)
    table = jnp.transpose(basis_table, (2, 3, 1, 0)).reshape(basis * taps, support, n_o)
    operands = [states.reshape(rows, lons, chans), cotangent.reshape(rows, lons, chans), table,
                offsets.reshape(1, n_o), widths.reshape(1, n_o), mixing,
                place, expand, own, spread, tap]
    hbm = pl.BlockSpec(memory_space=pltpu.HBM)
    dma = pltpu.SemaphoreType.DMA
    out, grad_states, grad_mix = pl.pallas_call(
        functools.partial(kernel, n_dp, n_lat),
        out_shape=(
            jax.ShapeDtypeStruct((rows, lons, chans), BF),
            jax.ShapeDtypeStruct((rows, lons, chans), BF),
            jax.ShapeDtypeStruct((deep, chans), BF),
        ),
        in_specs=[hbm] * 11,
        out_specs=(hbm, hbm, hbm),
        scratch_shapes=[pltpu.VMEM((rows, lons, chans), BF)] * 2 + [dma((3,))] + [pltpu.VMEM(x.shape, x.dtype) for x in operands] + [
            dma((len(operands),)),
            pltpu.VMEM((hops, wrapped, chans), BF),
            pltpu.VMEM((hops, wrapped, chans), BF),
            pltpu.VMEM((basis * taps, 256), F32),
            pltpu.VMEM(tap.shape[1:], BF),
            pltpu.VMEM(tap.shape[1:], BF),
            pltpu.VMEM((deep, chans), BF),
            pltpu.VMEM((cells, deep), BF),
            pltpu.VMEM((deep, chans), BF),
            pltpu.VMEM((n_plane, piece, chans), BF),
            pltpu.VMEM((piece, chans), BF),
            pltpu.VMEM((n_rest, piece, chans), BF),
            pltpu.VMEM((piece, chans), BF),
            pltpu.VMEM((deep, chans), BF),
            dma((2, 6)), dma((2, 6)),
            dma((n_plane,)), dma((n_plane,)),
            dma((n_rest,)), dma((n_rest,)),
            dma((n_plane,)), dma((n_plane,)),
        ],
        compiler_params=pltpu.CompilerParams(
            collective_id=0, has_side_effects=True, vmem_limit_bytes=63 * 1024 * 1024),
        cost_estimate=pl.CostEstimate(
            flops=2 * cells * deep * (3 * chans + 2 * 28 * taps),
            bytes_accessed=8 * cells * chans, transcendentals=0),
    )(*operands)
    cell_count = samples * n_dp * rows * n_lat * lons
    scale = 1.0 / math.sqrt(cell_count)
    out, grad_states, grad_mixing = pl.pallas_call(
        functools.partial(finish, scale),
        out_shape=(
            jax.ShapeDtypeStruct((rows, lons, chans), BF),
            jax.ShapeDtypeStruct((rows, lons, chans), BF),
            jax.ShapeDtypeStruct((deep, chans), F32),
        ),
        in_specs=[hbm] * 3,
        out_specs=(hbm, hbm, hbm),
        scratch_shapes=[pltpu.VMEM((deep, chans), BF), pltpu.VMEM((deep, chans), F32),
                        dma((4,))],
        compiler_params=pltpu.CompilerParams(vmem_limit_bytes=63 * 1024 * 1024),
    )(out, grad_states, grad_mix)
    shape = states.shape
    return (out.reshape(shape), grad_states.reshape(shape),
            grad_mixing.reshape(basis, chans, chans))


def solution(mesh):
    n_dp, n_lat = mesh.shape["dp"], mesh.shape["lat"]
    in_specs = (P("dp", "lat", None, None), P(), P(), P(), P(), P("dp", "lat", None, None))
    out_specs = (P("dp", "lat", None, None), P("dp", "lat", None, None), P())
    return jax.shard_map(functools.partial(shards, n_dp, n_lat), mesh=mesh, in_specs=in_specs,
                         out_specs=out_specs, check_vma=False)
```

```python
import functools
import math

import numpy as np
import jax
import jax.numpy as jnp
from jax import lax
from jax.experimental import pallas as pl
from jax.experimental.pallas import tpu as pltpu
from jax.sharding import PartitionSpec as P

HALO = 12
LB = 4
PLANE_DP = 2
PLANE_LAT = 4
PARTS = 3
MESH = pl.DeviceIdType.MESH
BF = jnp.bfloat16
F32 = jnp.float32


def dot(a, b):
    return jnp.dot(a, b, preferred_element_type=F32)


def structure(rows, basis, taps):
    ext = rows + 2 * HALO
    hops = ext // rows
    win = LB + taps - 1
    place = np.full((8, 256), -100000, np.int32)
    for r in range(rows):
        for e in range(ext):
            p = r * ext + e
            place[0, p] = r
            place[1, p] = e - r - HALO
            place[0, 128 + p] = e - HALO
            place[1, 128 + p] = r + HALO - e
    band = basis * LB * rows
    expand = np.zeros((taps, band, basis * taps), np.float32)
    own = np.zeros((band, 256), np.float32)
    spread = np.zeros((128, hops * win * rows), np.float32)
    tap = np.zeros((taps, band, hops * win * rows), np.float32)
    for k in range(basis):
        for lp in range(LB):
            for r in range(rows):
                row = (k * LB + lp) * rows + r
                for t in range(taps):
                    expand[t, row, k * taps + t] = 1
                    for j in range(hops):
                        base = (j * win + lp + t) * rows
                        tap[t, row, base : base + rows] = 1
                own[row, r * ext : (r + 1) * ext] = 1
                own[row, 128 + r * ext : 128 + (r + 1) * ext] = 1
    for r in range(rows):
        for e in range(ext):
            for w in range(win):
                spread[r * ext + e, ((e // rows) * win + w) * rows + e % rows] = 1
    as_bf = lambda x: np.asarray(x, dtype=jnp.bfloat16)
    return place, as_bf(expand), as_bf(own), as_bf(spread), as_bf(tap)


def kernel(
    n_dp, n_lat,
    states_h, cot_h, table_h, offs_h, wids_h, mixing_h, place_h, expand_h, own_h, spread_h, tap_h,
    out_h, grad_states_h, grad_mix_h,
    out, grad_states, store,
    states, cot, table, offs, wids, mixing, place, expand, own, spread, tap, load,
    buf_s, buf_c, rt, band_f, band_a, mix_t, filt, send_a, recv_a, part_b, recv_b, chunk, full,
    halo_send, halo_recv, a_send, a_recv, b_send, b_recv, d_send, d_recv,
):
    rows, lons, chans = states.shape
    basis = mixing.shape[0]
    taps = table.shape[0] // basis
    hops = buf_s.shape[0]
    reach = hops // 2
    n_plane = PLANE_DP * PLANE_LAT
    n_rest = (n_dp // PLANE_DP) * (n_lat // PLANE_LAT)
    lat_rest = n_lat // PLANE_LAT
    dp = lax.axis_index("dp")
    lat = lax.axis_index("lat")
    g = (dp % PLANE_DP) * PLANE_LAT + lat % PLANE_LAT
    z = (dp // PLANE_DP) * lat_rest + lat // PLANE_LAT

    def plane_peer(m):
        h = (g + m) % n_plane
        return h, ((dp // PLANE_DP) * PLANE_DP + h // PLANE_LAT,
                   (lat // PLANE_LAT) * PLANE_LAT + h % PLANE_LAT)

    def rest_peer(m):
        h = (z + m) % n_rest
        return h, ((h // lat_rest) * PLANE_DP + dp % PLANE_DP,
                   (h % lat_rest) * PLANE_LAT + lat % PLANE_LAT)

    loads = [
        pltpu.make_async_copy(src, dst, load.at[i])
        for i, (src, dst) in enumerate((
            (states_h, states), (cot_h, cot), (place_h, place), (offs_h, offs), (wids_h, wids),
            (table_h, table), (expand_h, expand), (own_h, own), (spread_h, spread),
            (tap_h, tap), (mixing_h, mixing)))
    ]
    for copy in loads:
        copy.start()

    core = lat % 2
    to_sib = 1 - 2 * core
    third = 6 * core - 3

    def there(d):
        return (lat + d >= 0) & (lat + d < n_lat)

    barrier = pltpu.get_barrier_semaphore()
    pl.semaphore_signal(barrier, inc=1, device_id=(dp, lat + to_sib), device_id_type=MESH)
    for d in (2, -2, third):
        @pl.when(there(d))
        def _():
            pl.semaphore_signal(barrier, inc=1, device_id=(dp, lat + d), device_id_type=MESH)
    for m in range(1, n_plane):
        pl.semaphore_signal(barrier, inc=1, device_id=plane_peer(m)[1], device_id_type=MESH)
    for m in range(1, n_rest):
        pl.semaphore_signal(barrier, inc=1, device_id=rest_peer(m)[1], device_id_type=MESH)

    half = taps // 2
    wrapped = buf_s.shape[1]
    cells = rows * lons
    rows_log, lons_log = rows.bit_length() - 1, lons.bit_length() - 1
    r_i = lax.broadcasted_iota(jnp.int32, (wrapped, cells), 0)
    c_i = lax.broadcasted_iota(jnp.int32, (wrapped, cells), 1)
    turned = jnp.where(r_i >= half * rows, r_i - half * rows, r_i + cells - half * rows)
    turned = jnp.where(turned >= cells, turned - cells, turned)
    source = (turned & (rows - 1)) * lons + (turned >> rows_log)
    perm = (source == c_i).astype(F32).astype(BF)

    def hop(which, buf, kind):
        src, slot, d, got, sent_if, got_if = {
            0: (reach, reach - to_sib, to_sib, reach + to_sib, None, None),
            1: (reach, reach - 2, 2, reach - 2, there(2), there(-2)),
            2: (reach, reach + 2, -2, reach + 2, there(-2), there(2)),
            3: (reach, reach - third, third, reach + third, there(third), there(third)),
            4: (reach - 2, reach - 2 - to_sib, to_sib, reach - 2 + to_sib, there(-2),
                there(to_sib - 2)),
            5: (reach + 2, reach + 2 - to_sib, to_sib, reach + 2 + to_sib, there(2),
                there(to_sib + 2)),
        }[kind]

        def copy(at):
            return pltpu.make_async_remote_copy(
                src_ref=buf.at[src], dst_ref=buf.at[at], send_sem=halo_send.at[which, kind],
                recv_sem=halo_recv.at[which, kind], device_id=(dp, lat + d), device_id_type=MESH)

        def run(cond, f):
            if cond is None:
                f()
            else:
                pl.when(cond)(f)

        return (lambda: run(sent_if, lambda: copy(slot).start()),
                lambda: run(got_if, lambda: copy(got).wait_recv()),
                lambda: run(sent_if, lambda: copy(slot).wait_send()))

    loads[0].wait()
    buf_s[reach] = dot(perm, states[...].reshape(cells, chans)).astype(BF)
    near = 1 + sum(there(d).astype(jnp.int32) for d in (2, -2, third))
    pl.semaphore_wait(barrier, near + (n_plane - 1 + n_rest - 1))
    for kind in (1, 2, 3, 0):
        hop(0, buf_s, kind)[0]()
    loads[1].wait()
    buf_c[reach] = dot(perm, cot[...].reshape(cells, chans)).astype(BF)
    for buf in (buf_s, buf_c):
        for d in range(-reach, reach + 1):
            if d:
                @pl.when(jnp.logical_not(there(d)))
                def _():
                    buf[reach + d] = jnp.zeros(buf.shape[1:], BF)
    for copy in loads[2:]:
        copy.wait()

    first = lat * rows
    n_o = table.shape[2]
    support = table.shape[1]
    o_i = lax.broadcasted_iota(jnp.int32, (n_o, 256), 0)
    pick = (o_i == place[0:1, :] + first).astype(F32).astype(BF)
    both = jnp.concatenate(
        [jnp.broadcast_to(offs[...].astype(F32), (8, n_o)),
         jnp.broadcast_to(wids[...].astype(F32), (8, n_o))], axis=0).astype(BF)
    picked = dot(both, pick)
    slot = place[1:2, :].astype(F32) - picked[0:1, :]
    s_i = lax.broadcasted_iota(jnp.int32, (support, 256), 0).astype(F32)
    live = jnp.where((s_i == slot) & (s_i < picked[8:9, :]), 1.0, 0.0)
    for kt in range(basis * taps):
        rt[kt : kt + 1, :] = jnp.sum(dot(table[kt], pick) * live, axis=0, keepdims=True)
    entries = rt[...].astype(BF)

    def build(band, lanes, tap_of):
        acc = jnp.zeros(band.shape, F32)
        for t in range(taps):
            rows_t = (dot(expand[t], entries[:, lanes]) * own[:, lanes].astype(F32)).astype(BF)
            acc = acc + dot(rows_t, spread[...]) * tap[tap_of(t)].astype(F32)
        band[...] = acc.astype(BF)

    build(band_f, slice(0, 128), lambda t: t)

    step = LB * rows
    span = (LB + taps - 1) * rows
    n_blocks = lons // LB

    def filter_all(band, buf):
        for b in range(0, n_blocks, 2):
            window = jnp.concatenate(
                [jnp.concatenate([buf[j, (b + i) * step : (b + i) * step + span, :]
                                  for j in range(hops)], axis=0) for i in range(2)], axis=1)
            res = dot(band[...], window).astype(BF)
            for i in range(2):
                for k in range(basis):
                    filt[(b + i) * step : (b + i + 1) * step, k * chans : (k + 1) * chans] = (
                        res[k * step : (k + 1) * step, i * chans : (i + 1) * chans])

    u_r = lax.broadcasted_iota(jnp.int32, (cells, cells), 0)
    u_c = lax.broadcasted_iota(jnp.int32, (cells, cells), 1)
    unperm = ((u_r & (lons - 1)) * rows + (u_r >> lons_log) == u_c).astype(F32).astype(BF)

    def pass_on(which, buf):
        for kind in (1, 2):
            hop(which, buf, kind)[1]()
        for kind in (4, 5):
            hop(which, buf, kind)[0]()

    def wait_rest(which, buf):
        for kind in (0, 3, 4, 5):
            hop(which, buf, kind)[1]()

    def unpermuted(x, ref):
        ref[...] = dot(unperm, x.astype(BF)).astype(BF).reshape(ref.shape)

    stores = [pltpu.make_async_copy(src, dst, store.at[i]) for i, (src, dst) in enumerate(
        ((out, out_h), (grad_states, grad_states_h), (full, grad_mix_h)))]

    pass_on(0, buf_s)
    for kind in (1, 2, 3, 0):
        hop(1, buf_c, kind)[0]()
    wait_rest(0, buf_s)
    filter_all(band_f, buf_s)
    mid = half * rows
    cot_rows = buf_c[reach, mid : mid + cells, :]
    grad_t = dot(cot_rows.astype(F32).T.astype(BF), filt[...])
    for k in range(basis):
        send_a[k * chans : (k + 1) * chans, :] = grad_t[:, k * chans : (k + 1) * chans].T.astype(BF)
    piece = chunk.shape[0]
    cut = piece // PARTS

    def rows_of(owner, i):
        return pl.ds(pl.multiple_of(owner * piece + i * cut, 16), cut)

    def a_copy(m, i):
        h, peer = plane_peer(m)
        return pltpu.make_async_remote_copy(
            src_ref=send_a.at[rows_of(h, i)], dst_ref=recv_a.at[m, pl.ds(i * cut, cut)],
            send_sem=a_send.at[m, i], recv_sem=a_recv.at[m, i], device_id=peer,
            device_id_type=MESH)

    for i in range(PARTS):
        for m in range(1, n_plane):
            a_copy(m, i).start()

    pass_on(1, buf_c)
    unpermuted(dot(filt[...], mixing[...].reshape(basis * chans, chans)), out)
    stores[0].start()
    build(band_a, slice(128, 256), lambda t: taps - 1 - t)
    for k in range(basis):
        mix_t[k * chans : (k + 1) * chans, :] = mixing[k].astype(F32).T.astype(BF)

    def b_copy(m, owner, i):
        return pltpu.make_async_remote_copy(
            src_ref=part_b.at[pl.ds(i * cut, cut)], dst_ref=recv_b.at[owner, pl.ds(i * cut, cut)],
            send_sem=b_send.at[m, i], recv_sem=b_recv.at[m, i], device_id=rest_peer(m)[1],
            device_id_type=MESH)

    for i in range(PARTS):
        at = slice(i * cut, (i + 1) * cut)
        total = send_a[rows_of(g, i), :].astype(F32)
        for m in range(1, n_plane):
            a_copy(m, i).wait_recv()
        for m in range(1, n_plane):
            total = total + recv_a[m, at, :].astype(F32)
        part_b[at, :] = total.astype(BF)
        recv_b[z, at, :] = total.astype(BF)
        for m in range(1, n_rest):
            b_copy(m, z, i).start()

    wait_rest(1, buf_c)
    filter_all(band_a, buf_c)

    def d_copy(m, owner, i):
        return pltpu.make_async_remote_copy(
            src_ref=chunk.at[pl.ds(i * cut, cut)], dst_ref=full.at[rows_of(owner, i)],
            send_sem=d_send.at[m, i], recv_sem=d_recv.at[m, i], device_id=plane_peer(m)[1],
            device_id_type=MESH)

    for i in range(PARTS):
        at = slice(i * cut, (i + 1) * cut)
        for m in range(1, n_rest):
            b_copy(m, (z - m + n_rest) % n_rest, i).wait_recv()
        total = recv_b[0, at, :].astype(F32)
        for h in range(1, n_rest):
            total = total + recv_b[h, at, :].astype(F32)
        chunk[at, :] = total.astype(BF)
        full[rows_of(g, i), :] = total.astype(BF)
        for m in range(1, n_plane):
            d_copy(m, g, i).start()

    unpermuted(dot(filt[...], mix_t[...]), grad_states)
    stores[1].start()

    for i in range(PARTS):
        for m in range(1, n_plane):
            d_copy(m, (g - m + n_plane) % n_plane, i).wait_recv()
    stores[2].start()

    for which, buf in ((0, buf_s), (1, buf_c)):
        for kind in range(6):
            hop(which, buf, kind)[2]()
    for i in range(PARTS):
        for m in range(1, n_plane):
            a_copy(m, i).wait_send()
            d_copy(m, g, i).wait_send()
        for m in range(1, n_rest):
            b_copy(m, z, i).wait_send()
    for copy in stores:
        copy.wait()


def finish(scale, out_in, grad_in, mix_in, out, grad_states, grad_mix, first, second, held, wide,
           sems):
    deep = held.shape[0]
    cut = deep // PARTS
    reads, writes = [], []
    for i in range(PARTS):
        rows = pl.ds(i * cut, cut)
        reads.append(pltpu.make_async_copy(mix_in.at[rows], held.at[rows], sems.at[0, i]))
        writes.append(pltpu.make_async_copy(wide.at[rows], grad_mix.at[rows], sems.at[1, i]))
    for i, (src, via, dst) in enumerate(((out_in, first, out), (grad_in, second, grad_states))):
        reads.append(pltpu.make_async_copy(src, via, sems.at[0, PARTS + i]))
        writes.append(pltpu.make_async_copy(via, dst, sems.at[1, PARTS + i]))
    for copy in reads:
        copy.start()
    for i in range(PARTS + 2):
        reads[i].wait()
        if i < PARTS:
            wide[i * cut : (i + 1) * cut, :] = held[i * cut : (i + 1) * cut, :].astype(F32) * scale
        writes[i].start()
    for copy in writes:
        copy.wait()


def shards(n_dp, n_lat, states, basis_table, offsets, widths, mixing, cotangent):
    samples, rows, lons, chans = states.shape
    n_o, support, basis, taps = basis_table.shape
    hops = 1 + 2 * (HALO // rows)
    n_plane = PLANE_DP * PLANE_LAT
    n_rest = n_dp * n_lat // n_plane
    wrapped = (lons + taps - 1) * rows
    cells = rows * lons
    deep = basis * chans
    piece = deep // n_plane
    place, expand, own, spread, tap = structure(rows, basis, taps)
    table = jnp.transpose(basis_table, (2, 3, 1, 0)).reshape(basis * taps, support, n_o)
    operands = [states.reshape(rows, lons, chans), cotangent.reshape(rows, lons, chans), table,
                offsets.reshape(1, n_o), widths.reshape(1, n_o), mixing,
                place, expand, own, spread, tap]
    hbm = pl.BlockSpec(memory_space=pltpu.HBM)
    dma = pltpu.SemaphoreType.DMA
    out, grad_states, grad_mix = pl.pallas_call(
        functools.partial(kernel, n_dp, n_lat),
        out_shape=(
            jax.ShapeDtypeStruct((rows, lons, chans), BF),
            jax.ShapeDtypeStruct((rows, lons, chans), BF),
            jax.ShapeDtypeStruct((deep, chans), BF),
        ),
        in_specs=[hbm] * 11,
        out_specs=(hbm, hbm, hbm),
        scratch_shapes=[pltpu.VMEM((rows, lons, chans), BF)] * 2 + [dma((3,))] + [pltpu.VMEM(x.shape, x.dtype) for x in operands] + [
            dma((len(operands),)),
            pltpu.VMEM((hops, wrapped, chans), BF),
            pltpu.VMEM((hops, wrapped, chans), BF),
            pltpu.VMEM((basis * taps, 256), F32),
            pltpu.VMEM(tap.shape[1:], BF),
            pltpu.VMEM(tap.shape[1:], BF),
            pltpu.VMEM((deep, chans), BF),
            pltpu.VMEM((cells, deep), BF),
            pltpu.VMEM((deep, chans), BF),
            pltpu.VMEM((n_plane, piece, chans), BF),
            pltpu.VMEM((piece, chans), BF),
            pltpu.VMEM((n_rest, piece, chans), BF),
            pltpu.VMEM((piece, chans), BF),
            pltpu.VMEM((deep, chans), BF),
            dma((2, 6)), dma((2, 6)),
            dma((n_plane, PARTS)), dma((n_plane, PARTS)),
            dma((n_rest, PARTS)), dma((n_rest, PARTS)),
            dma((n_plane, PARTS)), dma((n_plane, PARTS)),
        ],
        compiler_params=pltpu.CompilerParams(
            collective_id=0, has_side_effects=True, vmem_limit_bytes=63 * 1024 * 1024),
        cost_estimate=pl.CostEstimate(
            flops=2 * cells * deep * (3 * chans + 2 * 28 * taps),
            bytes_accessed=8 * cells * chans, transcendentals=0),
    )(*operands)
    cell_count = samples * n_dp * rows * n_lat * lons
    scale = 1.0 / math.sqrt(cell_count)
    out, grad_states, grad_mixing = pl.pallas_call(
        functools.partial(finish, scale),
        out_shape=(
            jax.ShapeDtypeStruct((rows, lons, chans), BF),
            jax.ShapeDtypeStruct((rows, lons, chans), BF),
            jax.ShapeDtypeStruct((deep, chans), F32),
        ),
        in_specs=[hbm] * 3,
        out_specs=(hbm, hbm, hbm),
        scratch_shapes=[pltpu.VMEM((rows, lons, chans), BF)] * 2 + [
            pltpu.VMEM((deep, chans), BF), pltpu.VMEM((deep, chans), F32), dma((2, PARTS + 2))],
        compiler_params=pltpu.CompilerParams(vmem_limit_bytes=63 * 1024 * 1024),
    )(out, grad_states, grad_mix)
    shape = states.shape
    return (out.reshape(shape), grad_states.reshape(shape),
            grad_mixing.reshape(basis, chans, chans))


def solution(mesh):
    n_dp, n_lat = mesh.shape["dp"], mesh.shape["lat"]
    in_specs = (P("dp", "lat", None, None), P(), P(), P(), P(), P("dp", "lat", None, None))
    out_specs = (P("dp", "lat", None, None), P("dp", "lat", None, None), P())
    return jax.shard_map(functools.partial(shards, n_dp, n_lat), mesh=mesh, in_specs=in_specs,
                         out_specs=out_specs, check_vma=False)
```

```python
import functools
import math

import numpy as np
import jax
import jax.numpy as jnp
from jax import lax
from jax.experimental import pallas as pl
from jax.experimental.pallas import tpu as pltpu
from jax.sharding import PartitionSpec as P

HALO = 12
LB = 4
PLANE_DP = 2
PLANE_LAT = 4
PARTS = 1
WRITES = 3
MESH = pl.DeviceIdType.MESH
BF = jnp.bfloat16
F32 = jnp.float32


def dot(a, b):
    return jnp.dot(a, b, preferred_element_type=F32)


def structure(rows, basis, taps):
    ext = rows + 2 * HALO
    hops = ext // rows
    win = LB + taps - 1
    place = np.full((8, 256), -100000, np.int32)
    for r in range(rows):
        for e in range(ext):
            p = r * ext + e
            place[0, p] = r
            place[1, p] = e - r - HALO
            place[0, 128 + p] = e - HALO
            place[1, 128 + p] = r + HALO - e
    band = basis * LB * rows
    expand = np.zeros((taps, band, basis * taps), np.float32)
    own = np.zeros((band, 256), np.float32)
    spread = np.zeros((128, hops * win * rows), np.float32)
    tap = np.zeros((taps, band, hops * win * rows), np.float32)
    for k in range(basis):
        for lp in range(LB):
            for r in range(rows):
                row = (k * LB + lp) * rows + r
                for t in range(taps):
                    expand[t, row, k * taps + t] = 1
                    for j in range(hops):
                        base = (j * win + lp + t) * rows
                        tap[t, row, base : base + rows] = 1
                own[row, r * ext : (r + 1) * ext] = 1
                own[row, 128 + r * ext : 128 + (r + 1) * ext] = 1
    for r in range(rows):
        for e in range(ext):
            for w in range(win):
                spread[r * ext + e, ((e // rows) * win + w) * rows + e % rows] = 1
    as_bf = lambda x: np.asarray(x, dtype=jnp.bfloat16)
    return place, as_bf(expand), as_bf(own), as_bf(spread), as_bf(tap)


def kernel(
    n_dp, n_lat,
    states_h, cot_h, table_h, offs_h, wids_h, mixing_h, place_h, expand_h, own_h, spread_h, tap_h,
    out_h, grad_states_h, grad_mix_h,
    out, grad_states, cot_t, store,
    states, cot, table, offs, wids, mixing, place, expand, own, spread, tap, load,
    buf_s, buf_c, rt, band_f, band_a, mix_t, filt, send_a, recv_a, part_b, recv_b, chunk, full,
    halo_send, halo_recv, a_send, a_recv, b_send, b_recv, d_send, d_recv,
):
    rows, lons, chans = states.shape
    basis = mixing.shape[0]
    taps = table.shape[0] // basis
    hops = buf_s.shape[0]
    reach = hops // 2
    n_plane = PLANE_DP * PLANE_LAT
    n_rest = (n_dp // PLANE_DP) * (n_lat // PLANE_LAT)
    lat_rest = n_lat // PLANE_LAT
    dp = lax.axis_index("dp")
    lat = lax.axis_index("lat")
    g = (dp % PLANE_DP) * PLANE_LAT + lat % PLANE_LAT
    z = (dp // PLANE_DP) * lat_rest + lat // PLANE_LAT

    def plane_peer(m):
        h = (g + m) % n_plane
        return h, ((dp // PLANE_DP) * PLANE_DP + h // PLANE_LAT,
                   (lat // PLANE_LAT) * PLANE_LAT + h % PLANE_LAT)

    def rest_peer(m):
        h = (z + m) % n_rest
        return h, ((h // lat_rest) * PLANE_DP + dp % PLANE_DP,
                   (h % lat_rest) * PLANE_LAT + lat % PLANE_LAT)

    loads = [
        pltpu.make_async_copy(src, dst, load.at[i])
        for i, (src, dst) in enumerate((
            (states_h, states), (cot_h, cot), (place_h, place), (offs_h, offs), (wids_h, wids),
            (table_h, table), (expand_h, expand), (own_h, own), (spread_h, spread),
            (tap_h, tap), (mixing_h, mixing)))
    ]
    for copy in loads:
        copy.start()

    core = lat % 2
    to_sib = 1 - 2 * core
    third = 6 * core - 3

    def there(d):
        return (lat + d >= 0) & (lat + d < n_lat)

    barrier = pltpu.get_barrier_semaphore()
    pl.semaphore_signal(barrier, inc=1, device_id=(dp, lat + to_sib), device_id_type=MESH)
    for d in (2, -2, third):
        @pl.when(there(d))
        def _():
            pl.semaphore_signal(barrier, inc=1, device_id=(dp, lat + d), device_id_type=MESH)
    for m in range(1, n_plane):
        pl.semaphore_signal(barrier, inc=1, device_id=plane_peer(m)[1], device_id_type=MESH)
    for m in range(1, n_rest):
        pl.semaphore_signal(barrier, inc=1, device_id=rest_peer(m)[1], device_id_type=MESH)

    half = taps // 2
    wrapped = buf_s.shape[1]
    cells = rows * lons
    rows_log, lons_log = rows.bit_length() - 1, lons.bit_length() - 1
    r_i = lax.broadcasted_iota(jnp.int32, (wrapped, cells), 0)
    c_i = lax.broadcasted_iota(jnp.int32, (wrapped, cells), 1)
    turned = jnp.where(r_i >= half * rows, r_i - half * rows, r_i + cells - half * rows)
    turned = jnp.where(turned >= cells, turned - cells, turned)
    source = (turned & (rows - 1)) * lons + (turned >> rows_log)
    perm = (source == c_i).astype(F32).astype(BF)

    head = (lons // 2 + taps - 1) * rows
    halves = (((0, head), (head, wrapped - head)), ((0, wrapped),))

    def hop(which, buf, kind, part):
        src, slot, d, got, sent_if, got_if = {
            0: (reach, reach - to_sib, to_sib, reach + to_sib, None, None),
            1: (reach, reach - 2, 2, reach - 2, there(2), there(-2)),
            2: (reach, reach + 2, -2, reach + 2, there(-2), there(2)),
            3: (reach, reach - third, third, reach + third, there(third), there(third)),
            4: (reach - 2, reach - 2 - to_sib, to_sib, reach - 2 + to_sib, there(-2),
                there(to_sib - 2)),
            5: (reach + 2, reach + 2 - to_sib, to_sib, reach + 2 + to_sib, there(2),
                there(to_sib + 2)),
        }[kind]

        span_of = pl.ds(*halves[which][part])

        def copy(at):
            return pltpu.make_async_remote_copy(
                src_ref=buf.at[src, span_of], dst_ref=buf.at[at, span_of],
                send_sem=halo_send.at[which, kind, part], recv_sem=halo_recv.at[which, kind, part],
                device_id=(dp, lat + d), device_id_type=MESH)

        def run(cond, f):
            if cond is None:
                f()
            else:
                pl.when(cond)(f)

        return (lambda: run(sent_if, lambda: copy(slot).start()),
                lambda: run(got_if, lambda: copy(got).wait_recv()),
                lambda: run(sent_if, lambda: copy(slot).wait_send()))

    loads[0].wait()
    buf_s[reach] = dot(perm, states[...].reshape(cells, chans)).astype(BF)
    near = 1 + sum(there(d).astype(jnp.int32) for d in (2, -2, third))
    pl.semaphore_wait(barrier, near + (n_plane - 1 + n_rest - 1))
    for part in range(2):
        for kind in (1, 2, 3, 0):
            hop(0, buf_s, kind, part)[0]()
    loads[1].wait()
    buf_c[reach] = dot(perm, cot[...].reshape(cells, chans)).astype(BF)
    for buf in (buf_s, buf_c):
        for d in range(-reach, reach + 1):
            if d:
                @pl.when(jnp.logical_not(there(d)))
                def _():
                    buf[reach + d] = jnp.zeros(buf.shape[1:], BF)
    for copy in loads[2:]:
        copy.wait()

    first = lat * rows
    n_o = table.shape[2]
    support = table.shape[1]
    o_i = lax.broadcasted_iota(jnp.int32, (n_o, 256), 0)
    pick = (o_i == place[0:1, :] + first).astype(F32).astype(BF)
    both = jnp.concatenate(
        [jnp.broadcast_to(offs[...].astype(F32), (8, n_o)),
         jnp.broadcast_to(wids[...].astype(F32), (8, n_o))], axis=0).astype(BF)
    picked = dot(both, pick)
    slot = place[1:2, :].astype(F32) - picked[0:1, :]
    s_i = lax.broadcasted_iota(jnp.int32, (support, 256), 0).astype(F32)
    live = jnp.where((s_i == slot) & (s_i < picked[8:9, :]), 1.0, 0.0)
    for kt in range(basis * taps):
        rt[kt : kt + 1, :] = jnp.sum(dot(table[kt], pick) * live, axis=0, keepdims=True)
    entries = rt[...].astype(BF)

    def build(band, lanes, tap_of):
        acc = jnp.zeros(band.shape, F32)
        for t in range(taps):
            rows_t = (dot(expand[t], entries[:, lanes]) * own[:, lanes].astype(F32)).astype(BF)
            acc = acc + dot(rows_t, spread[...]) * tap[tap_of(t)].astype(F32)
        band[...] = acc.astype(BF)

    build(band_f, slice(0, 128), lambda t: t)
    build(band_a, slice(128, 256), lambda t: taps - 1 - t)
    for k in range(basis):
        mix_t[k * chans : (k + 1) * chans, :] = mixing[k].astype(F32).T.astype(BF)
    mid = half * rows
    cot_t[...] = buf_c[reach, mid : mid + cells, :].astype(F32).T.astype(BF)

    step = LB * rows
    span = (LB + taps - 1) * rows
    n_blocks = lons // LB

    def filter_all(band, buf, begin, end):
        for b in range(begin, end, 2):
            window = jnp.concatenate(
                [jnp.concatenate([buf[j, (b + i) * step : (b + i) * step + span, :]
                                  for j in range(hops)], axis=0) for i in range(2)], axis=1)
            res = dot(band[...], window).astype(BF)
            for i in range(2):
                for k in range(basis):
                    filt[(b + i) * step : (b + i + 1) * step, k * chans : (k + 1) * chans] = (
                        res[k * step : (k + 1) * step, i * chans : (i + 1) * chans])

    u_r = lax.broadcasted_iota(jnp.int32, (cells, cells), 0)
    u_c = lax.broadcasted_iota(jnp.int32, (cells, cells), 1)
    unperm = ((u_r & (lons - 1)) * rows + (u_r >> lons_log) == u_c).astype(F32).astype(BF)

    def pass_on(which, buf, part):
        for kind in (1, 2):
            hop(which, buf, kind, part)[1]()
        for kind in (4, 5):
            hop(which, buf, kind, part)[0]()

    def wait_rest(which, buf, part):
        for kind in (0, 3, 4, 5):
            hop(which, buf, kind, part)[1]()

    def unpermuted(x, ref):
        ref[...] = dot(unperm, x.astype(BF)).astype(BF).reshape(ref.shape)

    stores = [pltpu.make_async_copy(src, dst, store.at[i]) for i, (src, dst) in enumerate(
        ((out, out_h), (grad_states, grad_states_h), (full, grad_mix_h)))]

    pass_on(0, buf_s, 0)
    wait_rest(0, buf_s, 0)
    filter_all(band_f, buf_s, 0, n_blocks // 2)
    pass_on(0, buf_s, 1)
    for kind in (1, 2, 3, 0):
        hop(1, buf_c, kind, 0)[0]()
    wait_rest(0, buf_s, 1)
    filter_all(band_f, buf_s, n_blocks // 2, n_blocks)
    grad_t = dot(cot_t[...], filt[...])
    for k in range(basis):
        send_a[k * chans : (k + 1) * chans, :] = grad_t[:, k * chans : (k + 1) * chans].T.astype(BF)
    piece = chunk.shape[0]
    cut = piece // PARTS

    def rows_of(owner, i):
        return pl.ds(pl.multiple_of(owner * piece + i * cut, 16), cut)

    def a_copy(m, i):
        h, peer = plane_peer(m)
        return pltpu.make_async_remote_copy(
            src_ref=send_a.at[rows_of(h, i)], dst_ref=recv_a.at[m, pl.ds(i * cut, cut)],
            send_sem=a_send.at[m, i], recv_sem=a_recv.at[m, i], device_id=peer,
            device_id_type=MESH)

    for i in range(PARTS):
        for m in range(1, n_plane):
            a_copy(m, i).start()

    pass_on(1, buf_c, 0)
    unpermuted(dot(filt[...], mixing[...].reshape(basis * chans, chans)), out)
    stores[0].start()

    def b_copy(m, owner, i):
        return pltpu.make_async_remote_copy(
            src_ref=part_b.at[pl.ds(i * cut, cut)], dst_ref=recv_b.at[owner, pl.ds(i * cut, cut)],
            send_sem=b_send.at[m, i], recv_sem=b_recv.at[m, i], device_id=rest_peer(m)[1],
            device_id_type=MESH)

    for i in range(PARTS):
        at = slice(i * cut, (i + 1) * cut)
        total = send_a[rows_of(g, i), :].astype(F32)
        for m in range(1, n_plane):
            a_copy(m, i).wait_recv()
        for m in range(1, n_plane):
            total = total + recv_a[m, at, :].astype(F32)
        part_b[at, :] = total.astype(BF)
        recv_b[z, at, :] = total.astype(BF)
        for m in range(1, n_rest):
            b_copy(m, z, i).start()

    wait_rest(1, buf_c, 0)
    filter_all(band_a, buf_c, 0, n_blocks)

    def d_copy(m, owner, i):
        return pltpu.make_async_remote_copy(
            src_ref=chunk.at[pl.ds(i * cut, cut)], dst_ref=full.at[rows_of(owner, i)],
            send_sem=d_send.at[m, i], recv_sem=d_recv.at[m, i], device_id=plane_peer(m)[1],
            device_id_type=MESH)

    for i in range(PARTS):
        at = slice(i * cut, (i + 1) * cut)
        for m in range(1, n_rest):
            b_copy(m, (z - m + n_rest) % n_rest, i).wait_recv()
        total = recv_b[0, at, :].astype(F32)
        for h in range(1, n_rest):
            total = total + recv_b[h, at, :].astype(F32)
        chunk[at, :] = total.astype(BF)
        full[rows_of(g, i), :] = total.astype(BF)
        for m in range(1, n_plane):
            d_copy(m, g, i).start()

    unpermuted(dot(filt[...], mix_t[...]), grad_states)
    stores[1].start()

    for i in range(PARTS):
        for m in range(1, n_plane):
            d_copy(m, (g - m + n_plane) % n_plane, i).wait_recv()
    stores[2].start()

    for which, buf in ((0, buf_s), (1, buf_c)):
        for part in range(len(halves[which])):
            for kind in range(6):
                hop(which, buf, kind, part)[2]()
    for i in range(PARTS):
        for m in range(1, n_plane):
            a_copy(m, i).wait_send()
            d_copy(m, g, i).wait_send()
        for m in range(1, n_rest):
            b_copy(m, z, i).wait_send()
    for copy in stores:
        copy.wait()


def finish(scale, out_in, grad_in, mix_in, out, grad_states, grad_mix, first, second, held, wide,
           sems):
    deep = held.shape[0]
    cut = deep // WRITES
    reads, writes = [], []
    for i in range(WRITES):
        rows = pl.ds(i * cut, cut)
        reads.append(pltpu.make_async_copy(mix_in.at[rows], held.at[rows], sems.at[0, i]))
        writes.append(pltpu.make_async_copy(wide.at[rows], grad_mix.at[rows], sems.at[1, i]))
    for i, (src, via, dst) in enumerate(((out_in, first, out), (grad_in, second, grad_states))):
        reads.append(pltpu.make_async_copy(src, via, sems.at[0, WRITES + i]))
        writes.append(pltpu.make_async_copy(via, dst, sems.at[1, WRITES + i]))
    for copy in reads:
        copy.start()
    for i in range(WRITES + 2):
        reads[i].wait()
        if i < WRITES:
            wide[i * cut : (i + 1) * cut, :] = held[i * cut : (i + 1) * cut, :].astype(F32) * scale
        writes[i].start()
    for copy in writes:
        copy.wait()


def shards(n_dp, n_lat, states, basis_table, offsets, widths, mixing, cotangent):
    samples, rows, lons, chans = states.shape
    n_o, support, basis, taps = basis_table.shape
    hops = 1 + 2 * (HALO // rows)
    n_plane = PLANE_DP * PLANE_LAT
    n_rest = n_dp * n_lat // n_plane
    wrapped = (lons + taps - 1) * rows
    cells = rows * lons
    deep = basis * chans
    piece = deep // n_plane
    place, expand, own, spread, tap = structure(rows, basis, taps)
    table = jnp.transpose(basis_table, (2, 3, 1, 0)).reshape(basis * taps, support, n_o)
    operands = [states.reshape(rows, lons, chans), cotangent.reshape(rows, lons, chans), table,
                offsets.reshape(1, n_o), widths.reshape(1, n_o), mixing,
                place, expand, own, spread, tap]
    hbm = pl.BlockSpec(memory_space=pltpu.HBM)
    dma = pltpu.SemaphoreType.DMA
    out, grad_states, grad_mix = pl.pallas_call(
        functools.partial(kernel, n_dp, n_lat),
        out_shape=(
            jax.ShapeDtypeStruct((rows, lons, chans), BF),
            jax.ShapeDtypeStruct((rows, lons, chans), BF),
            jax.ShapeDtypeStruct((deep, chans), BF),
        ),
        in_specs=[hbm] * 11,
        out_specs=(hbm, hbm, hbm),
        scratch_shapes=[pltpu.VMEM((rows, lons, chans), BF)] * 2 + [
            pltpu.VMEM((chans, cells), BF), dma((3,))] + [pltpu.VMEM(x.shape, x.dtype) for x in operands] + [
            dma((len(operands),)),
            pltpu.VMEM((hops, wrapped, chans), BF),
            pltpu.VMEM((hops, wrapped, chans), BF),
            pltpu.VMEM((basis * taps, 256), F32),
            pltpu.VMEM(tap.shape[1:], BF),
            pltpu.VMEM(tap.shape[1:], BF),
            pltpu.VMEM((deep, chans), BF),
            pltpu.VMEM((cells, deep), BF),
            pltpu.VMEM((deep, chans), BF),
            pltpu.VMEM((n_plane, piece, chans), BF),
            pltpu.VMEM((piece, chans), BF),
            pltpu.VMEM((n_rest, piece, chans), BF),
            pltpu.VMEM((piece, chans), BF),
            pltpu.VMEM((deep, chans), BF),
            dma((2, 6, 2)), dma((2, 6, 2)),
            dma((n_plane, PARTS)), dma((n_plane, PARTS)),
            dma((n_rest, PARTS)), dma((n_rest, PARTS)),
            dma((n_plane, PARTS)), dma((n_plane, PARTS)),
        ],
        compiler_params=pltpu.CompilerParams(
            collective_id=0, has_side_effects=True, vmem_limit_bytes=63 * 1024 * 1024),
        cost_estimate=pl.CostEstimate(
            flops=2 * cells * deep * (3 * chans + 2 * 28 * taps),
            bytes_accessed=8 * cells * chans, transcendentals=0),
    )(*operands)
    cell_count = samples * n_dp * rows * n_lat * lons
    scale = 1.0 / math.sqrt(cell_count)
    out, grad_states, grad_mixing = pl.pallas_call(
        functools.partial(finish, scale),
        out_shape=(
            jax.ShapeDtypeStruct((rows, lons, chans), BF),
            jax.ShapeDtypeStruct((rows, lons, chans), BF),
            jax.ShapeDtypeStruct((deep, chans), F32),
        ),
        in_specs=[hbm] * 3,
        out_specs=(hbm, hbm, hbm),
        scratch_shapes=[pltpu.VMEM((rows, lons, chans), BF)] * 2 + [
            pltpu.VMEM((deep, chans), BF), pltpu.VMEM((deep, chans), F32), dma((2, WRITES + 2))],
        compiler_params=pltpu.CompilerParams(vmem_limit_bytes=63 * 1024 * 1024),
    )(out, grad_states, grad_mix)
    shape = states.shape
    return (out.reshape(shape), grad_states.reshape(shape),
            grad_mixing.reshape(basis, chans, chans))


def solution(mesh):
    n_dp, n_lat = mesh.shape["dp"], mesh.shape["lat"]
    in_specs = (P("dp", "lat", None, None), P(), P(), P(), P(), P("dp", "lat", None, None))
    out_specs = (P("dp", "lat", None, None), P("dp", "lat", None, None), P())
    return jax.shard_map(functools.partial(shards, n_dp, n_lat), mesh=mesh, in_specs=in_specs,
                         out_specs=out_specs, check_vma=False)
```

```python
import functools
import math

import numpy as np
import jax
import jax.numpy as jnp
from jax import lax
from jax.experimental import pallas as pl
from jax.experimental.pallas import tpu as pltpu
from jax.sharding import PartitionSpec as P

HALO = 12
LB = 4
PLANE_DP = 2
PLANE_LAT = 4
PARTS = 1
WRITES = 3
MESH = pl.DeviceIdType.MESH
BF = jnp.bfloat16
F32 = jnp.float32


def dot(a, b):
    return jnp.dot(a, b, preferred_element_type=F32)


def structure(rows, basis, taps):
    ext = rows + 2 * HALO
    hops = ext // rows
    win = LB + taps - 1
    place = np.full((8, 256), -100000, np.int32)
    for r in range(rows):
        for e in range(ext):
            p = r * ext + e
            place[0, p] = r
            place[1, p] = e - r - HALO
            place[0, 128 + p] = e - HALO
            place[1, 128 + p] = r + HALO - e
    band = basis * LB * rows
    expand = np.zeros((taps, band, basis * taps), np.float32)
    own = np.zeros((band, 256), np.float32)
    spread = np.zeros((128, hops * win * rows), np.float32)
    tap = np.zeros((taps, band, hops * win * rows), np.float32)
    for k in range(basis):
        for lp in range(LB):
            for r in range(rows):
                row = (k * LB + lp) * rows + r
                for t in range(taps):
                    expand[t, row, k * taps + t] = 1
                    for j in range(hops):
                        base = (j * win + lp + t) * rows
                        tap[t, row, base : base + rows] = 1
                own[row, r * ext : (r + 1) * ext] = 1
                own[row, 128 + r * ext : 128 + (r + 1) * ext] = 1
    for r in range(rows):
        for e in range(ext):
            for w in range(win):
                spread[r * ext + e, ((e // rows) * win + w) * rows + e % rows] = 1
    as_bf = lambda x: np.asarray(x, dtype=jnp.bfloat16)
    return place, as_bf(expand), as_bf(own), as_bf(spread), as_bf(tap)


def kernel(
    n_dp, n_lat,
    states_h, cot_h, table_h, offs_h, wids_h, mixing_h, place_h, expand_h, own_h, spread_h, tap_h,
    out_h, grad_states_h, grad_mix_h,
    out, grad_states, store,
    states, cot, table, offs, wids, mixing, place, expand, own, spread, tap, load,
    buf_s, buf_c, rt, band_f, band_a, mix_t, filt, send_a, recv_a, part_b, recv_b, chunk, full,
    halo_send, halo_recv, a_send, a_recv, b_send, b_recv, d_send, d_recv,
):
    rows, lons, chans = states.shape
    basis = mixing.shape[0]
    taps = table.shape[0] // basis
    hops = buf_s.shape[0]
    reach = hops // 2
    n_plane = PLANE_DP * PLANE_LAT
    n_rest = (n_dp // PLANE_DP) * (n_lat // PLANE_LAT)
    lat_rest = n_lat // PLANE_LAT
    dp = lax.axis_index("dp")
    lat = lax.axis_index("lat")
    g = (dp % PLANE_DP) * PLANE_LAT + lat % PLANE_LAT
    z = (dp // PLANE_DP) * lat_rest + lat // PLANE_LAT

    def plane_peer(m):
        h = (g + m) % n_plane
        return h, ((dp // PLANE_DP) * PLANE_DP + h // PLANE_LAT,
                   (lat // PLANE_LAT) * PLANE_LAT + h % PLANE_LAT)

    def rest_peer(m):
        h = (z + m) % n_rest
        return h, ((h // lat_rest) * PLANE_DP + dp % PLANE_DP,
                   (h % lat_rest) * PLANE_LAT + lat % PLANE_LAT)

    loads = [
        pltpu.make_async_copy(src, dst, load.at[i])
        for i, (src, dst) in enumerate((
            (states_h, states), (cot_h, cot), (place_h, place), (offs_h, offs), (wids_h, wids),
            (table_h, table), (expand_h, expand), (own_h, own), (spread_h, spread),
            (tap_h, tap), (mixing_h, mixing)))
    ]
    for copy in loads:
        copy.start()

    core = lat % 2
    to_sib = 1 - 2 * core
    third = 6 * core - 3

    def there(d):
        return (lat + d >= 0) & (lat + d < n_lat)

    barrier = pltpu.get_barrier_semaphore()
    pl.semaphore_signal(barrier, inc=1, device_id=(dp, lat + to_sib), device_id_type=MESH)
    for d in (2, -2, third):
        @pl.when(there(d))
        def _():
            pl.semaphore_signal(barrier, inc=1, device_id=(dp, lat + d), device_id_type=MESH)
    for m in range(1, n_plane):
        pl.semaphore_signal(barrier, inc=1, device_id=plane_peer(m)[1], device_id_type=MESH)
    for m in range(1, n_rest):
        pl.semaphore_signal(barrier, inc=1, device_id=rest_peer(m)[1], device_id_type=MESH)

    half = taps // 2
    wrapped = buf_s.shape[1]
    cells = rows * lons
    rows_log, lons_log = rows.bit_length() - 1, lons.bit_length() - 1
    r_i = lax.broadcasted_iota(jnp.int32, (wrapped, cells), 0)
    c_i = lax.broadcasted_iota(jnp.int32, (wrapped, cells), 1)
    turned = jnp.where(r_i >= half * rows, r_i - half * rows, r_i + cells - half * rows)
    turned = jnp.where(turned >= cells, turned - cells, turned)
    source = (turned & (rows - 1)) * lons + (turned >> rows_log)
    perm = (source == c_i).astype(F32).astype(BF)

    def hop(which, buf, kind):
        src, slot, d, got, sent_if, got_if = {
            0: (reach, reach - to_sib, to_sib, reach + to_sib, None, None),
            1: (reach, reach - 2, 2, reach - 2, there(2), there(-2)),
            2: (reach, reach + 2, -2, reach + 2, there(-2), there(2)),
            3: (reach, reach - third, third, reach + third, there(third), there(third)),
            4: (reach - 2, reach - 2 - to_sib, to_sib, reach - 2 + to_sib, there(-2),
                there(to_sib - 2)),
            5: (reach + 2, reach + 2 - to_sib, to_sib, reach + 2 + to_sib, there(2),
                there(to_sib + 2)),
        }[kind]

        def copy(at):
            return pltpu.make_async_remote_copy(
                src_ref=buf.at[src], dst_ref=buf.at[at], send_sem=halo_send.at[which, kind],
                recv_sem=halo_recv.at[which, kind], device_id=(dp, lat + d), device_id_type=MESH)

        def run(cond, f):
            if cond is None:
                f()
            else:
                pl.when(cond)(f)

        return (lambda: run(sent_if, lambda: copy(slot).start()),
                lambda: run(got_if, lambda: copy(got).wait_recv()),
                lambda: run(sent_if, lambda: copy(slot).wait_send()))

    loads[0].wait()
    buf_s[reach] = dot(perm, states[...].reshape(cells, chans)).astype(BF)
    near = 1 + sum(there(d).astype(jnp.int32) for d in (2, -2, third))
    pl.semaphore_wait(barrier, near + (n_plane - 1 + n_rest - 1))
    for kind in (1, 2, 3, 0):
        hop(0, buf_s, kind)[0]()
    loads[1].wait()
    buf_c[reach] = dot(perm, cot[...].reshape(cells, chans)).astype(BF)
    for buf in (buf_s, buf_c):
        for d in range(-reach, reach + 1):
            if d:
                @pl.when(jnp.logical_not(there(d)))
                def _():
                    buf[reach + d] = jnp.zeros(buf.shape[1:], BF)
    for copy in loads[2:]:
        copy.wait()

    first = lat * rows
    n_o = table.shape[2]
    support = table.shape[1]
    o_i = lax.broadcasted_iota(jnp.int32, (n_o, 256), 0)
    pick = (o_i == place[0:1, :] + first).astype(F32).astype(BF)
    both = jnp.concatenate(
        [jnp.broadcast_to(offs[...].astype(F32), (8, n_o)),
         jnp.broadcast_to(wids[...].astype(F32), (8, n_o))], axis=0).astype(BF)
    picked = dot(both, pick)
    slot = place[1:2, :].astype(F32) - picked[0:1, :]
    s_i = lax.broadcasted_iota(jnp.int32, (support, 256), 0).astype(F32)
    live = jnp.where((s_i == slot) & (s_i < picked[8:9, :]), 1.0, 0.0)
    def build(band, lanes, tap_of):
        for kt in range(basis * taps):
            rt[kt : kt + 1, lanes] = jnp.sum(
                dot(table[kt], pick[:, lanes]) * live[:, lanes], axis=0, keepdims=True)
        entries = rt[:, lanes].astype(BF)
        acc = jnp.zeros(band.shape, F32)
        for t in range(taps):
            rows_t = (dot(expand[t], entries) * own[:, lanes].astype(F32)).astype(BF)
            acc = acc + dot(rows_t, spread[...]) * tap[tap_of(t)].astype(F32)
        band[...] = acc.astype(BF)

    build(band_f, slice(0, 128), lambda t: t)

    step = LB * rows
    span = (LB + taps - 1) * rows
    n_blocks = lons // LB

    def filter_all(band, buf):
        for b in range(0, n_blocks, 2):
            window = jnp.concatenate(
                [jnp.concatenate([buf[j, (b + i) * step : (b + i) * step + span, :]
                                  for j in range(hops)], axis=0) for i in range(2)], axis=1)
            res = dot(band[...], window).astype(BF)
            for i in range(2):
                for k in range(basis):
                    filt[(b + i) * step : (b + i + 1) * step, k * chans : (k + 1) * chans] = (
                        res[k * step : (k + 1) * step, i * chans : (i + 1) * chans])

    def pass_on(which, buf):
        for kind in (1, 2):
            hop(which, buf, kind)[1]()
        for kind in (4, 5):
            hop(which, buf, kind)[0]()

    def wait_rest(which, buf):
        for kind in (0, 3, 4, 5):
            hop(which, buf, kind)[1]()

    def unpermuted(x, ref):
        ref[...] = dot(unperm, x.astype(BF)).astype(BF).reshape(ref.shape)

    stores = [pltpu.make_async_copy(src, dst, store.at[i]) for i, (src, dst) in enumerate(
        ((out, out_h), (grad_states, grad_states_h), (full, grad_mix_h)))]

    pass_on(0, buf_s)
    for kind in (1, 2, 3, 0):
        hop(1, buf_c, kind)[0]()
    wait_rest(0, buf_s)
    filter_all(band_f, buf_s)
    mid = half * rows
    cot_rows = buf_c[reach, mid : mid + cells, :]
    grad_t = dot(cot_rows.astype(F32).T.astype(BF), filt[...])
    for k in range(basis):
        send_a[k * chans : (k + 1) * chans, :] = grad_t[:, k * chans : (k + 1) * chans].T.astype(BF)
    piece = chunk.shape[0]
    cut = piece // PARTS

    def rows_of(owner, i):
        return pl.ds(pl.multiple_of(owner * piece + i * cut, 16), cut)

    def a_copy(m, i):
        h, peer = plane_peer(m)
        return pltpu.make_async_remote_copy(
            src_ref=send_a.at[rows_of(h, i)], dst_ref=recv_a.at[m, pl.ds(i * cut, cut)],
            send_sem=a_send.at[m, i], recv_sem=a_recv.at[m, i], device_id=peer,
            device_id_type=MESH)

    for i in range(PARTS):
        for m in range(1, n_plane):
            a_copy(m, i).start()

    u_r = lax.broadcasted_iota(jnp.int32, (cells, cells), 0)
    u_c = lax.broadcasted_iota(jnp.int32, (cells, cells), 1)
    unperm = ((u_r & (lons - 1)) * rows + (u_r >> lons_log) == u_c).astype(F32).astype(BF)
    pass_on(1, buf_c)
    unpermuted(dot(filt[...], mixing[...].reshape(basis * chans, chans)), out)
    stores[0].start()
    build(band_a, slice(128, 256), lambda t: taps - 1 - t)
    for k in range(basis):
        mix_t[k * chans : (k + 1) * chans, :] = mixing[k].astype(F32).T.astype(BF)

    def b_copy(m, owner, i):
        return pltpu.make_async_remote_copy(
            src_ref=part_b.at[pl.ds(i * cut, cut)], dst_ref=recv_b.at[owner, pl.ds(i * cut, cut)],
            send_sem=b_send.at[m, i], recv_sem=b_recv.at[m, i], device_id=rest_peer(m)[1],
            device_id_type=MESH)

    for i in range(PARTS):
        at = slice(i * cut, (i + 1) * cut)
        total = send_a[rows_of(g, i), :].astype(F32)
        for m in range(1, n_plane):
            a_copy(m, i).wait_recv()
        for m in range(1, n_plane):
            total = total + recv_a[m, at, :].astype(F32)
        part_b[at, :] = total.astype(BF)
        recv_b[z, at, :] = total.astype(BF)
        for m in range(1, n_rest):
            b_copy(m, z, i).start()

    wait_rest(1, buf_c)
    filter_all(band_a, buf_c)

    def d_copy(m, owner, i):
        return pltpu.make_async_remote_copy(
            src_ref=chunk.at[pl.ds(i * cut, cut)], dst_ref=full.at[rows_of(owner, i)],
            send_sem=d_send.at[m, i], recv_sem=d_recv.at[m, i], device_id=plane_peer(m)[1],
            device_id_type=MESH)

    for i in range(PARTS):
        at = slice(i * cut, (i + 1) * cut)
        for m in range(1, n_rest):
            b_copy(m, (z - m + n_rest) % n_rest, i).wait_recv()
        total = recv_b[0, at, :].astype(F32)
        for h in range(1, n_rest):
            total = total + recv_b[h, at, :].astype(F32)
        chunk[at, :] = total.astype(BF)
        full[rows_of(g, i), :] = total.astype(BF)
        for m in range(1, n_plane):
            d_copy(m, g, i).start()

    unpermuted(dot(filt[...], mix_t[...]), grad_states)
    stores[1].start()

    for i in range(PARTS):
        for m in range(1, n_plane):
            d_copy(m, (g - m + n_plane) % n_plane, i).wait_recv()
    stores[2].start()

    for which, buf in ((0, buf_s), (1, buf_c)):
        for kind in range(6):
            hop(which, buf, kind)[2]()
    for i in range(PARTS):
        for m in range(1, n_plane):
            a_copy(m, i).wait_send()
            d_copy(m, g, i).wait_send()
        for m in range(1, n_rest):
            b_copy(m, z, i).wait_send()
    for copy in stores:
        copy.wait()


def finish(scale, out_in, grad_in, mix_in, out, grad_states, grad_mix, first, second, held, wide,
           sems):
    deep = held.shape[0]
    cut = deep // WRITES
    reads, writes = [], []
    for i in range(WRITES):
        rows = pl.ds(i * cut, cut)
        reads.append(pltpu.make_async_copy(mix_in.at[rows], held.at[rows], sems.at[0, i]))
        writes.append(pltpu.make_async_copy(wide.at[rows], grad_mix.at[rows], sems.at[1, i]))
    for i, (src, via, dst) in enumerate(((out_in, first, out), (grad_in, second, grad_states))):
        reads.append(pltpu.make_async_copy(src, via, sems.at[0, WRITES + i]))
        writes.append(pltpu.make_async_copy(via, dst, sems.at[1, WRITES + i]))
    for copy in reads:
        copy.start()
    for i in range(WRITES + 2):
        reads[i].wait()
        if i < WRITES:
            wide[i * cut : (i + 1) * cut, :] = held[i * cut : (i + 1) * cut, :].astype(F32) * scale
        writes[i].start()
    for copy in writes:
        copy.wait()


def shards(n_dp, n_lat, states, basis_table, offsets, widths, mixing, cotangent):
    samples, rows, lons, chans = states.shape
    n_o, support, basis, taps = basis_table.shape
    hops = 1 + 2 * (HALO // rows)
    n_plane = PLANE_DP * PLANE_LAT
    n_rest = n_dp * n_lat // n_plane
    wrapped = (lons + taps - 1) * rows
    cells = rows * lons
    deep = basis * chans
    piece = deep // n_plane
    place, expand, own, spread, tap = structure(rows, basis, taps)
    table = jnp.transpose(basis_table, (2, 3, 1, 0)).reshape(basis * taps, support, n_o)
    operands = [states.reshape(rows, lons, chans), cotangent.reshape(rows, lons, chans), table,
                offsets.reshape(1, n_o), widths.reshape(1, n_o), mixing,
                place, expand, own, spread, tap]
    hbm = pl.BlockSpec(memory_space=pltpu.HBM)
    dma = pltpu.SemaphoreType.DMA
    out, grad_states, grad_mix = pl.pallas_call(
        functools.partial(kernel, n_dp, n_lat),
        out_shape=(
            jax.ShapeDtypeStruct((rows, lons, chans), BF),
            jax.ShapeDtypeStruct((rows, lons, chans), BF),
            jax.ShapeDtypeStruct((deep, chans), BF),
        ),
        in_specs=[hbm] * 11,
        out_specs=(hbm, hbm, hbm),
        scratch_shapes=[pltpu.VMEM((rows, lons, chans), BF)] * 2 + [dma((3,))] + [pltpu.VMEM(x.shape, x.dtype) for x in operands] + [
            dma((len(operands),)),
            pltpu.VMEM((hops, wrapped, chans), BF),
            pltpu.VMEM((hops, wrapped, chans), BF),
            pltpu.VMEM((basis * taps, 256), F32),
            pltpu.VMEM(tap.shape[1:], BF),
            pltpu.VMEM(tap.shape[1:], BF),
            pltpu.VMEM((deep, chans), BF),
            pltpu.VMEM((cells, deep), BF),
            pltpu.VMEM((deep, chans), BF),
            pltpu.VMEM((n_plane, piece, chans), BF),
            pltpu.VMEM((piece, chans), BF),
            pltpu.VMEM((n_rest, piece, chans), BF),
            pltpu.VMEM((piece, chans), BF),
            pltpu.VMEM((deep, chans), BF),
            dma((2, 6)), dma((2, 6)),
            dma((n_plane, PARTS)), dma((n_plane, PARTS)),
            dma((n_rest, PARTS)), dma((n_rest, PARTS)),
            dma((n_plane, PARTS)), dma((n_plane, PARTS)),
        ],
        compiler_params=pltpu.CompilerParams(
            collective_id=0, has_side_effects=True, vmem_limit_bytes=63 * 1024 * 1024),
        cost_estimate=pl.CostEstimate(
            flops=2 * cells * deep * (3 * chans + 2 * 28 * taps),
            bytes_accessed=8 * cells * chans, transcendentals=0),
    )(*operands)
    cell_count = samples * n_dp * rows * n_lat * lons
    scale = 1.0 / math.sqrt(cell_count)
    out, grad_states, grad_mixing = pl.pallas_call(
        functools.partial(finish, scale),
        out_shape=(
            jax.ShapeDtypeStruct((rows, lons, chans), BF),
            jax.ShapeDtypeStruct((rows, lons, chans), BF),
            jax.ShapeDtypeStruct((deep, chans), F32),
        ),
        in_specs=[hbm] * 3,
        out_specs=(hbm, hbm, hbm),
        scratch_shapes=[pltpu.VMEM((rows, lons, chans), BF)] * 2 + [
            pltpu.VMEM((deep, chans), BF), pltpu.VMEM((deep, chans), F32), dma((2, WRITES + 2))],
        compiler_params=pltpu.CompilerParams(vmem_limit_bytes=63 * 1024 * 1024),
    )(out, grad_states, grad_mix)
    shape = states.shape
    return (out.reshape(shape), grad_states.reshape(shape),
            grad_mixing.reshape(basis, chans, chans))


def solution(mesh):
    n_dp, n_lat = mesh.shape["dp"], mesh.shape["lat"]
    in_specs = (P("dp", "lat", None, None), P(), P(), P(), P(), P("dp", "lat", None, None))
    out_specs = (P("dp", "lat", None, None), P("dp", "lat", None, None), P())
    return jax.shard_map(functools.partial(shards, n_dp, n_lat), mesh=mesh, in_specs=in_specs,
                         out_specs=out_specs, check_vma=False)
```
